32 devices in a mesh: replica: 4 (over z), tensor: 2 (over core), section: 4 (over y, x).
Axes of the slice: x: 2, y: 2, z: 4, core: 2. Of those that a mesh axis runs over, the one named last changes fastest.
Arguments:
- weight: bfloat16 [4096, 1024], P('section', 'tensor'), may hold values from -3 to 3
- grads: bfloat16 [4, 4096, 1024], P('replica', 'section', 'tensor'), may hold values from -83 to 83
- error: bfloat16 [4, 4096, 1024], P('replica', 'section', 'tensor'), may hold values from -3 to 3
- momentum: float32 [4096, 1024], P('section', 'tensor'), may hold values from -6 to 6
- basis: float32 [1024, 32], P('tensor'), may hold values from -6 to 6
- gram_root: float32 [32, 32], replicated, may hold values from -1 to 1
- gain: float32 [2, 4096], P(None, ('tensor', 'section')), may hold values from 0.5 to 1.5
- gain_momentum: float32 [2, 4096], P(None, ('tensor', 'section')), may hold values from -3 to 3
- gain_grads: float32 [4, 2, 4096], P('replica', None, ('tensor', 'section')), may hold values from -176 to 176
Outputs:
- new_weight: bfloat16 [4096, 1024], P(None, 'tensor')
- new_error: bfloat16 [4, 4096, 1024], P('replica', 'section', 'tensor')
- new_momentum: float32 [4096, 1024], P('section', 'tensor')
- new_gain: float32 [2, 4096], replicated
- new_gain_momentum: float32 [2, 4096], P(None, ('tensor', 'section'))
The draws below stay inside these ranges and needn't reach their ends.
All inputs are finite; a program needn't handle non-finite values.
Results may differ from the reference program's by a relative error of at most 0.0004.
Values may be sent and summed in bfloat16 or wider, within the bound.
No kernel may reach another device: no remote copies, remote signals or barrier semaphores. Data moves between devices by JAX's collectives and lax.ppermute only.
A program may use at most 64 MiB of HBM per device.

```python
import math
import jax
import jax.numpy as jnp
from jax import lax

D = 4096
KV = 1024
RANK = 32
N_REPLICA = 4


def draw_grads(key, part):
    keys = jax.random.split(jax.random.fold_in(key, 11), 4)
    rise_rows = 1.0 + 2.0 * jnp.arange(D, dtype=jnp.float32) / max(D - 1, 1)
    rise_cols = 1.0 + 2.0 * jnp.arange(KV, dtype=jnp.float32) / max(KV - 1, 1)
    rise_reps = 1.0 + 2.0 * jnp.arange(N_REPLICA, dtype=jnp.float32) / max(N_REPLICA - 1, 1)
    row_scale = jnp.exp(jax.random.uniform(keys[0], (D,), jnp.float32, 0.0, math.log(10.0))) * rise_rows
    col_scale = jnp.exp(jax.random.uniform(keys[1], (KV,), jnp.float32, 0.0, math.log(10.0))) * rise_cols
    own = jnp.clip(jax.random.normal(keys[3], (N_REPLICA, D, KV), jnp.float32), -6.0, 6.0)
    common = jnp.clip(jax.random.normal(keys[2], (D, KV), jnp.float32), -6.0, 6.0)
    mixed = 0.3 * common + own
    values = mixed * row_scale[None, :, None] * col_scale[None, None, :] * rise_reps[:, None, None] / 256.0
    return values.astype(jnp.bfloat16)


def draw_gram_root(key, part):
    keys = jax.random.split(jax.random.fold_in(key, 23), 2)
    diag = 2.0 * jnp.exp(jax.random.uniform(keys[0], (RANK,), jnp.float32, 0.0, math.log(2.0)))
    noise = jnp.clip(jax.random.normal(keys[1], (RANK, RANK), jnp.float32), -4.0, 4.0)
    sym = (noise + noise.T) * (0.5 / math.sqrt(RANK))
    whole = sym + jnp.eye(RANK, dtype=jnp.float32) * diag[:, None]
    return (whole / (2.0 * math.sqrt(D * KV))).astype(jnp.float32)


def draw_gain_grads(key, part):
    keys = jax.random.split(jax.random.fold_in(key, 37), 3)
    rise_cols = 1.0 + 2.0 * jnp.arange(D, dtype=jnp.float32) / max(D - 1, 1)
    rise_reps = 1.0 + 2.0 * jnp.arange(N_REPLICA, dtype=jnp.float32) / max(N_REPLICA - 1, 1)
    col_scale = jnp.exp(jax.random.uniform(keys[0], (2, D), jnp.float32, 0.0, math.log(10.0))) * rise_cols[None]
    own = jnp.clip(jax.random.normal(keys[2], (N_REPLICA, 2, D), jnp.float32), -6.0, 6.0)
    common = jnp.clip(jax.random.normal(keys[1], (2, D), jnp.float32), -6.0, 6.0)
    mixed = 0.3 * common + own
    return (mixed * col_scale[None] * rise_reps[:, None, None] / 4.0).astype(jnp.float32)


def levels(key, dims, pieces, least, high):
    def one(position, blocks):
        draws = jax.random.uniform(jax.random.fold_in(jax.random.fold_in(key, 6), position), (blocks,), jnp.float32, least / len(pieces), high / len(pieces))
        return jnp.repeat(jnp.exp(draws), dims[position] // blocks).reshape((-1,) + (1,) * (len(dims) - position - 1))

    level = one(*pieces[0])
    for cut in pieces[1:]:
        level = level * one(*cut)
    return level


def gaussian(key, dims, spread, bound, cuts=(), kind=jnp.bfloat16):
    result = spread * jax.random.normal(key, dims, jnp.float32)
    if cuts:
        result = result * levels(key, dims, cuts, -0.22, 0.18)
    return jnp.clip(result, -bound, bound).astype(kind)


def setup_inputs(seed: int = 0) -> dict:
    key_list = jax.random.split(jax.random.key(seed), 10)
    return {
        "weight": gaussian(key_list[0], (D, KV), 0.5, 3.0, ((0, 4), (1, 2))),
        "grads": draw_grads(jax.random.fold_in(key_list[9], 71), 0),
        "error": gaussian(key_list[2], (N_REPLICA, D, KV), 0.5, 3.0, ((0, 4), (1, 4), (2, 2))),
        "momentum": gaussian(key_list[3], (D, KV), 1.0, 6.0, ((0, 4), (1, 2)), jnp.float32),
        "basis": gaussian(key_list[4], (KV, RANK), 1.0, 6.0, ((0, 2),), jnp.float32),
        "gram_root": draw_gram_root(jax.random.fold_in(key_list[9], 71), 0),
        "gain": jnp.clip(1.0 + 0.1 * jax.random.normal(key_list[6], (2, D), jnp.float32), 0.5, 1.5),
        "gain_momentum": gaussian(key_list[7], (2, D), 0.5, 3.0, ((1, 8),), jnp.float32),
        "gain_grads": draw_gain_grads(jax.random.fold_in(key_list[9], 71), 0),
    }


def reference(weight, grads, error, momentum, basis, gram_root, gain, gain_momentum, gain_grads):
    highest = lax.Precision.HIGHEST

    def left_term(total, pair):
        merged = pair[0].astype(jnp.float32) + pair[1].astype(jnp.float32)
        return (total + jnp.dot(merged, basis, precision=highest), None)
    lowp_total, unused = lax.scan(left_term, jnp.zeros((D, RANK), jnp.float32), (grads, error))
    lowp = lowp_total / N_REPLICA
    ortho = jnp.dot(lowp, gram_root, precision=highest)

    def right_term(total, pair):
        merged = pair[0].astype(jnp.float32) + pair[1].astype(jnp.float32)
        return (total + jnp.dot(merged.T, ortho, precision=highest), None)
    basis_total, unused = lax.scan(right_term, jnp.zeros((KV, RANK), jnp.float32), (grads, error))
    newbasis = basis_total / N_REPLICA
    approx = jnp.dot(ortho, newbasis.T, precision=highest)
    merged_all = grads.astype(jnp.float32) + error.astype(jnp.float32)
    new_error = (merged_all - approx[None]).astype(jnp.bfloat16)
    scale = lax.rsqrt(jnp.mean(approx * approx) + 1e-06)
    update = scale * approx
    new_momentum = 0.9 * momentum + update
    new_weight = (weight.astype(jnp.float32) - 0.05 * (update + 0.9 * new_momentum)).astype(jnp.bfloat16)
    gain_mean = lax.optimization_barrier(jnp.sum(gain_grads, axis=0)) / N_REPLICA
    new_gain_momentum = 0.9 * gain_momentum + gain_mean
    new_gain = gain - 0.02 * (gain_mean + 0.9 * new_gain_momentum)
    return (new_weight, new_error, new_momentum, new_gain, new_gain_momentum)
```

```python
import jax
import jax.numpy as jnp
from jax import lax
from jax.sharding import PartitionSpec as P

HIGHEST = lax.Precision.HIGHEST


def swap(x, axis, distance):
    count = lax.axis_size(axis)
    return lax.ppermute(x, axis, [(i, i ^ distance) for i in range(count)])


def total(x, axis):
    count = lax.axis_size(axis)
    distance = 1
    while distance < count:
        if count // distance >= 4:
            a = swap(x, axis, distance)
            b = swap(x, axis, 2 * distance)
            c = swap(x, axis, 3 * distance)
            x = (x + a) + (b + c)
            distance *= 4
        else:
            x = x + swap(x, axis, distance)
            distance *= 2
    return x


def gathered(x, axis):
    count = lax.axis_size(axis)
    me = lax.axis_index(axis)
    half = x.shape[0] // 2
    if count == 4:
        one = swap(x, axis, 1)
        two = swap(x, axis, 2)
        low = swap(two[:half], axis, 1)
        high = swap(one[half:], axis, 2)
        parts = [x, one, two, jnp.concatenate([low, high], axis=0)]
    else:
        parts = [x] + [swap(x, axis, d) for d in range(1, count)]
    rows = x.shape[0]
    out = jnp.zeros((count * rows,) + x.shape[1:], x.dtype)
    for distance, part in enumerate(parts):
        out = lax.dynamic_update_slice(out, part, ((me ^ distance) * rows, 0))
    return out


def on_device(weight, grads, error, momentum, basis, gram_root, gain, gain_momentum, gain_grads):
    replicas = lax.axis_size("replica")
    tensors = lax.axis_size("tensor")
    sections = lax.axis_size("section")
    tensor = lax.axis_index("tensor")
    section = lax.axis_index("section")
    rows, cols = weight.shape
    rank = basis.shape[1]
    merged = grads[0].astype(jnp.float32) + error[0].astype(jnp.float32)
    lowp_term = lax.dot_general(basis, merged, (((0,), (1,)), ((), ())), precision=HIGHEST)
    half = rows // 2
    kept = lax.dynamic_slice(lowp_term, (0, tensor * half), (rank, half))
    given = lax.dynamic_slice(lowp_term, (0, (1 - tensor) * half), (rank, half))
    pair = kept + swap(given, "tensor", 1)
    pair = jnp.concatenate([pair, gain_grads[0]], axis=0)
    pair = total(pair, "replica")
    gain_mean = pair[rank:] / replicas
    mine = pair[:rank]
    other = swap(mine, "tensor", 1)
    first = jnp.where(tensor == 0, mine, other)
    second = jnp.where(tensor == 0, other, mine)
    lowp = jnp.concatenate([first, second], axis=1) / replicas
    ortho = lax.dot_general(gram_root, lowp, (((0,), (0,)), ((), ())), precision=HIGHEST)
    new_gain_momentum = 0.9 * gain_momentum + gain_mean
    local_gain = gain - 0.02 * (gain_mean + 0.9 * new_gain_momentum)
    basis_term = jnp.dot(ortho, merged, precision=HIGHEST)
    gram = lax.dot_general(ortho, ortho, (((1,), (1,)), ((), ())), precision=HIGHEST)
    joined = jnp.concatenate([basis_term, gram], axis=1)
    joined = total(total(joined, "section"), "replica") / replicas
    newbasis = joined[:, :cols]
    gram = joined[:, cols:]
    approx = lax.dot_general(ortho, newbasis, (((0,), (0,)), ((), ())), precision=HIGHEST)
    merged = grads[0].astype(jnp.float32) + error[0].astype(jnp.float32)
    new_error = (merged - approx).astype(jnp.bfloat16)[None]
    right = lax.dot_general(newbasis, newbasis, (((1,), (1,)), ((), ())), precision=HIGHEST)
    right = right + swap(right, "tensor", 1)
    entries = rows * cols * tensors * sections
    scale = lax.rsqrt(jnp.sum((gram / entries) * right) + 1e-06)
    update = scale * approx
    new_momentum = 0.9 * momentum + update
    local_weight = (weight.astype(jnp.float32) - 0.05 * (update + 0.9 * new_momentum)).astype(
        jnp.bfloat16
    )
    new_weight = gathered(local_weight, "section")
    wide = gathered(local_gain, "section")
    wide = wide.reshape(sections, 2, cols).transpose(1, 0, 2).reshape(2, sections * cols)
    other = swap(wide, "tensor", 1)
    new_gain = jnp.where(
        tensor == 0,
        jnp.concatenate([wide, other], axis=1),
        jnp.concatenate([other, wide], axis=1),
    )
    return (new_weight, new_error, new_momentum, new_gain, new_gain_momentum)


def solution(mesh):
    placed = (
        P("section", "tensor"),
        P("replica", "section", "tensor"),
        P("replica", "section", "tensor"),
        P("section", "tensor"),
        P("tensor", None),
        P(),
        P(None, ("tensor", "section")),
        P(None, ("tensor", "section")),
        P("replica", None, ("tensor", "section")),
    )
    return jax.shard_map(
        on_device,
        mesh=mesh,
        in_specs=placed,
        out_specs=(
            P(None, "tensor"),
            P("replica", "section", "tensor"),
            P("section", "tensor"),
            P(),
            P(None, ("tensor", "section")),
        ),
        check_vma=False,
    )
```

```python
import functools

import jax
import jax.numpy as jnp
from jax import lax
from jax.experimental import pallas as pl
from jax.experimental.pallas import tpu as pltpu
from jax.sharding import PartitionSpec as P

HIGHEST = lax.Precision.HIGHEST
F32 = jnp.float32
BF16 = jnp.bfloat16
KEEP = 0.05 * 0.9 * 0.9
MOVE = 0.05 * (1.0 + 0.9)
EARLY = 11
BLOCKS = 4
WHOLE = pl.BlockSpec(memory_space=pltpu.VMEM)
SCALAR = pl.BlockSpec(memory_space=pltpu.SMEM)
ANYWHERE = pl.BlockSpec(memory_space=pl.ANY)
IN_HBM = pl.BlockSpec(memory_space=pltpu.HBM)
PARAMS = pltpu.CompilerParams(vmem_limit_bytes=16 * 2**20)


def hbm(x):
    return pltpu.with_memory_space_constraint(x, pltpu.HBM)


def swap(x, axis, distance):
    count = lax.axis_size(axis)
    return lax.ppermute(x, axis, [(i, i ^ distance) for i in range(count)])


def partners(x, axis):
    count = lax.axis_size(axis)
    while count > 4:
        count //= 2
        x = x + swap(x, axis, count)
    return [x] + [swap(x, axis, distance) for distance in range(1, count)]


def added(parts):
    while len(parts) > 1:
        parts = [a + b for a, b in zip(parts[::2], parts[1::2])]
    return parts[0]


def packed(square):
    step = 8
    return jnp.concatenate([square[i : i + step] for i in range(0, square.shape[0], step)], axis=1)


def pieces(x):
    one = x.astype(BF16)
    rest = x - one.astype(F32)
    two = rest.astype(BF16)
    three = (rest - two.astype(F32)).astype(BF16)
    return one, two, three


def dot(a, b, dims):
    return lax.dot_general(a, b, ((dims[0], dims[1]), ((), ())), preferred_element_type=F32)


def folded(x):
    rank = x.shape[0] // 3
    return x[:rank] + x[rank : 2 * rank] + x[2 * rank :]


def loaded(grads_any, error_any, grads_ref, error_ref, sems):
    rows = grads_any.shape[0]
    block = rows // BLOCKS
    copies = []
    for part in range(BLOCKS):
        span = pl.ds(part * block, block)
        copies.append((grads_any.at[span], grads_ref.at[span]))
        copies.append((error_any.at[span], error_ref.at[span]))
    copies = fetch(copies, sems)

    def blocks():
        for part in range(BLOCKS):
            copies[2 * part].wait()
            copies[2 * part + 1].wait()
            span = pl.ds(part * block, block)
            yield part, grads_ref[span, :], error_ref[span, :]

    return blocks


def left_kernel(basis_ref, grads_any, error_any, gains_ref, kept_ref, given_ref, grads_ref, error_ref, sems):
    blocks = loaded(grads_any, error_any, grads_ref, error_ref, sems)
    stack = jnp.concatenate(pieces(basis_ref[...]), axis=0)
    rank = basis_ref.shape[0]
    half = grads_ref.shape[0] // 2
    kept_ref[rank:, :] = jnp.concatenate([gains_ref[...], jnp.zeros((6, half), F32)], axis=0)
    terms = []
    for _, grads, error in blocks():
        terms.append(folded(dot(stack, grads, ((1,), (1,))) + dot(stack, error, ((1,), (1,)))))
    middle = BLOCKS // 2
    front = jnp.concatenate(terms[:middle], axis=1)
    back = jnp.concatenate(terms[middle:], axis=1)
    first = lax.axis_index("tensor") == 0
    kept_ref[:rank, :] = jnp.where(first, front, back)
    given_ref[...] = jnp.where(first, back, front)


def pair_kernel(kept_ref, other_ref, out_ref):
    rank = other_ref.shape[0]
    out_ref[:rank, :] = kept_ref[:rank, :] + other_ref[...]
    out_ref[rank:, :] = kept_ref[rank:, :]


def sum_kernel(replicas, *refs):
    *parts, gain_ref, gain_momentum_ref, mine_ref, new_gain_momentum_ref, tail_ref = refs
    mean = added([part[...] for part in parts]) / replicas
    rank = mine_ref.shape[0]
    mine_ref[...] = mean[:rank]
    gain_mean = mean[rank : rank + 2]
    new_gain_momentum = 0.9 * gain_momentum_ref[...] + gain_mean
    new_gain_momentum_ref[...] = new_gain_momentum
    new_gain = gain_ref[...] - 0.02 * (gain_mean + 0.9 * new_gain_momentum)
    tail_ref[...] = jnp.concatenate([new_gain[:, i * 128 : (i + 1) * 128] for i in range(4)], axis=0)


def right_kernel(mine_ref, other_ref, root_ref, grads_ref, error_ref, term_ref, gram_ref, ortho_ref):
    rank, half = mine_ref.shape
    first = lax.axis_index("tensor") == 0
    mine = mine_ref[...]
    other = other_ref[...]
    lowp = (jnp.where(first, mine, other), jnp.where(first, other, mine))
    orthos = [
        lax.dot_general(root_ref[...], x, (((0,), (0,)), ((), ())), precision=HIGHEST, preferred_element_type=F32)
        for x in lowp
    ]
    stacks = [jnp.concatenate(pieces(x), axis=0) for x in orthos]
    for part in range(2):
        ortho_ref[pl.ds(part * rank, rank), :] = orthos[part]
    gram = sum(
        lax.dot_general(x, x, (((1,), (1,)), ((), ())), precision=HIGHEST, preferred_element_type=F32) for x in orthos
    )
    gram_ref[...] = packed(gram)
    term = jnp.zeros((3 * rank, grads_ref.shape[1]), F32)
    for part, stack in enumerate(stacks):
        span = pl.ds(part * half, half)
        term += dot(stack, grads_ref[span, :], ((1,), (0,))) + dot(stack, error_ref[span, :], ((1,), (0,)))
    term_ref[...] = folded(term)


def middle_kernel(count, *refs):
    parts, (gram_ref, tail_ref, _, _, out_ref) = refs[:count], refs[count:]
    term = added([part[...] for part in parts])
    rank, cols = term.shape
    out_ref[:rank, :] = term
    out_ref[rank:, :128] = gram_ref[...]
    out_ref[rank:, 128:256] = tail_ref[...]
    out_ref[rank:, 256:] = jnp.zeros((8, cols - 256), F32)


def factor_kernel(replicas, *refs):
    *parts, newbasis_ref, gram_ref, right_ref, wide_ref = refs
    rank, cols = newbasis_ref.shape
    values = [part[...] for part in parts]
    mean = added(values)
    newbasis = mean[:rank] / replicas
    newbasis_ref[...] = newbasis
    right = lax.dot_general(newbasis, newbasis, (((1,), (1,)), ((), ())), precision=HIGHEST, preferred_element_type=F32)
    gram_ref[...] = mean[rank:, :128]
    right_ref[...] = packed(right)
    section = lax.axis_index("section")
    for distance, value in enumerate(values):
        gain = jnp.concatenate([value[rank + 2 * i : rank + 2 * i + 2, 128:256] for i in range(4)], axis=1)
        for place in range(len(values)):

            @pl.when(section == place ^ distance)
            def _(place=place, gain=gain):
                wide_ref[:, place * cols : (place + 1) * cols] = gain


def base_of(weight, momentum):
    return weight.astype(F32) - KEEP * momentum


def fetch(copies, sems):
    started = []
    for index, (source, target) in enumerate(copies):
        copy = pltpu.make_async_copy(source, target, sems.at[index])
        copy.start()
        started.append(copy)
    return started


def start_kernel(weight_any, momentum_any, x_early_any, y_early_any, late_any, weight_ref, momentum_ref, base_ref, sems):
    rows = weight_any.shape[0]
    early = x_early_any.shape[0]
    late = rows - early
    block = rows // BLOCKS
    copies = []
    for part in range(BLOCKS):
        span = pl.ds(part * block, block)
        copies.append((weight_any.at[span], weight_ref.at[span]))
        copies.append((momentum_any.at[span], momentum_ref.at[span]))
    copies = fetch(copies, sems)
    sent = []
    for part in range(BLOCKS):
        copies[2 * part].wait()
        copies[2 * part + 1].wait()
        start, stop = part * block, (part + 1) * block
        span = pl.ds(start, block)
        base_ref[span, :] = base_of(weight_ref[span, :], momentum_ref[span, :])
        for low, high, ref, shift in (
            (0, early, y_early_any, 0),
            (late, rows, x_early_any, late),
            (0, late, late_any, 0),
            (early, rows, late_any, early - late),
        ):
            low, high = max(low, start), min(high, stop)
            if low < high:
                source = base_ref.at[pl.ds(low, high - low)]
                target = ref.at[pl.ds(low - shift, high - low)]
                sent.append(pltpu.make_async_copy(source, target, sems.at[2 * BLOCKS + len(sent)]))
                sent[-1].start()
    for copy in sent:
        copy.wait()


def left_stack(ortho):
    one, two, three = pieces(ortho)
    return jnp.concatenate([one, one, two, one, two, three], axis=0)


def right_stack(newbasis):
    one, two, three = pieces(newbasis)
    return jnp.concatenate([one, two, one, three, two, one], axis=0)


def product(ortho, right):
    return dot(left_stack(ortho), right, ((0,), (0,)))


def moved(base, scale, approx):
    return (base - (MOVE * scale) * approx).astype(BF16)


def after_kernel(entries, newbasis_ref, gram_ref, mine_ref, other_ref, own_ref, x_left_ref, y_left_ref, late_any, x_early_ref, y_early_ref, to_x_ref, to_y_ref, scale_ref, section_ref, late_ref, sems):
    (copy,) = fetch([(late_any, late_ref)], sems)
    rank = newbasis_ref.shape[0]
    early = x_early_ref.shape[0]
    late = late_ref.shape[0] // 2
    half = (early + late) // 2
    skip = half - late
    squares = (gram_ref[...] / entries) * (mine_ref[...] + other_ref[...])
    mean = jnp.sum(jnp.sum(squares, axis=1, keepdims=True), axis=0, keepdims=True)
    scale = lax.rsqrt(mean + 1e-06)
    scale_ref[...] = jnp.broadcast_to(scale, scale_ref.shape)
    section_ref[0] = lax.axis_index("section")
    right = right_stack(newbasis_ref[...])
    to_x_ref[:half, :] = moved(y_early_ref[:half, :], scale, product(y_left_ref[:rank, :], right))
    to_y_ref[:half, :] = moved(x_early_ref[early - half :, :], scale, product(x_left_ref[rank:, :], right))
    copy.wait()
    to_x_ref[half:, :] = moved(late_ref[:late, :], scale, product(own_ref[:rank, :late], right))
    to_y_ref[half:, :] = moved(late_ref[late:, :], scale, product(own_ref[rank:, skip:], right))


def own_kernel(place_ref, scale_ref, newbasis_ref, own_ref, weight_ref, momentum_ref, grads_ref, error_ref, new_error_ref, new_momentum_ref, out_ref):
    del place_ref
    rank, cols = newbasis_ref.shape
    block = weight_ref.shape[0]
    step = pl.program_id(0)
    per = cols // block
    start = (step // per) * rank
    columns = pl.ds(pl.multiple_of((step % per) * block, block), block)
    scale = scale_ref[0:1, 0:1]
    ortho = own_ref[pl.ds(pl.multiple_of(start, rank), rank), columns]
    approx = product(ortho, right_stack(newbasis_ref[...]))
    merged = grads_ref[...].astype(F32) + error_ref[...].astype(F32)
    new_error_ref[...] = (merged - approx).astype(BF16)
    momentum = momentum_ref[...]
    new_momentum_ref[...] = 0.9 * momentum + scale * approx
    out_ref[...] = moved(base_of(weight_ref[...], momentum), scale, approx)


def near_kernel(scale_ref, newbasis_ref, x_left_ref, y_left_ref, x_early_ref, y_early_ref, held_ref, out_ref, done_ref, sems):
    del held_ref
    rank = newbasis_ref.shape[0]
    early = x_early_ref.shape[0]
    half = x_left_ref.shape[1]
    extra = early - half
    rows = 2 * half
    scale = scale_ref[0:1, 0:1]
    right = right_stack(newbasis_ref[...])
    section = lax.axis_index("section")
    x_side = (section ^ 1) * rows
    y_side = (section ^ 2) * rows
    work = (
        (x_early_ref, 0, x_left_ref[:rank, half - extra :], extra, x_side + half - extra),
        (x_early_ref, extra, x_left_ref[rank:, :], half, x_side + half),
        (y_early_ref, 0, y_left_ref[:rank, :], half, y_side),
        (y_early_ref, half, y_left_ref[rank:, :extra], extra, y_side + half),
    )
    sent = []
    start = 0
    for index, (ref, begin, ortho, size, to) in enumerate(work):
        span = pl.ds(start, size)
        done_ref[span, :] = moved(ref[begin : begin + size, :], scale, product(ortho, right))
        to = pl.multiple_of(to, 64)
        copy = pltpu.make_async_copy(done_ref.at[span], out_ref.at[pl.ds(to, size)], sems.at[index])
        copy.start()
        sent.append(copy)
        start += size
    for copy in sent:
        copy.wait()


def settle_kernel(x_ref, y_ref, held_ref, out_ref, sems):
    del held_ref
    rows = out_ref.shape[0] // lax.axis_size("section")
    half = rows // 2
    late = x_ref.shape[0] - half
    section = lax.axis_index("section")
    x_side = (section ^ 1) * rows
    y_side = (section ^ 2) * rows
    across = (section ^ 3) * rows
    copies = []
    for ref, start, size, to in (
        (x_ref, 0, half, across),
        (x_ref, half, late, x_side),
        (y_ref, 0, half, across + half),
        (y_ref, half, late, y_side + rows - late),
    ):
        to = pl.multiple_of(to, 64)
        copies.append((ref.at[pl.ds(start, size), :], out_ref.at[pl.ds(to, size), :]))
    for copy in fetch(copies, sems):
        copy.wait()


def gain_kernel(wide_ref, other_ref, out_ref):
    cols = wide_ref.shape[1]
    first = lax.axis_index("tensor") == 0
    wide = wide_ref[...]
    other = other_ref[...]
    out_ref[:, :cols] = jnp.where(first, wide, other)
    out_ref[:, cols:] = jnp.where(first, other, wide)


def shape(dims, kind):
    return jax.ShapeDtypeStruct(dims, kind)


def cost(flops, size):
    return pl.CostEstimate(flops=flops, bytes_accessed=size, transcendentals=0)


def call(kernel, name, out_shape, in_specs, size, **more):
    out_specs = more.pop("out_specs", [WHOLE] * len(out_shape))
    return pl.pallas_call(
        kernel,
        out_shape=out_shape,
        in_specs=in_specs,
        out_specs=out_specs,
        compiler_params=PARAMS,
        name=name,
        cost_estimate=cost(0, size),
        **more,
    )


def on_device(weight, grads, error, momentum, basis, gram_root, gain, gain_momentum, gain_grads):
    replicas = lax.axis_size("replica")
    tensors = lax.axis_size("tensor")
    sections = lax.axis_size("section")
    rows, cols = weight.shape
    rank = basis.shape[1]
    half = rows // 2
    early = rows * EARLY // 16
    late = rows - early
    grads = hbm(grads[0])
    error = hbm(error[0])
    weight = hbm(weight)
    momentum = hbm(momentum)

    x_early, y_early, late_rows = call(
        start_kernel,
        "start",
        [pltpu.HBM((early, cols), F32)] * 2 + [pltpu.HBM((2 * late, cols), F32)],
        [IN_HBM] * 2,
        0,
        out_specs=[IN_HBM] * 3,
        scratch_shapes=[
            pltpu.VMEM((rows, cols), BF16),
            pltpu.VMEM((rows, cols), F32),
            pltpu.VMEM((rows, cols), F32),
            pltpu.SemaphoreType.DMA((6 * BLOCKS,)),
        ],
    )(weight, momentum)
    from_x = swap(x_early, "section", 1)
    from_y = swap(y_early, "section", 2)

    kept, given, held_grads, held_error = call(
        left_kernel,
        "left",
        [shape((rank + 8, half), F32), shape((rank, half), F32)] + [pltpu.VMEM((rows, cols), BF16)] * 2,
        [WHOLE, IN_HBM, IN_HBM, WHOLE],
        0,
        scratch_shapes=[pltpu.SemaphoreType.DMA((2 * BLOCKS,))],
    )(basis.T, grads, error, gain_grads[0])
    (pair,) = call(pair_kernel, "pair", [shape(kept.shape, F32)], [WHOLE] * 2, 0)(kept, swap(given, "tensor", 1))
    parts = partners(pair, "replica")
    mine, new_gain_momentum, tail = call(
        functools.partial(sum_kernel, replicas),
        "sum",
        [shape((rank, half), F32), shape((2, cols), F32), shape((8, 128), F32)],
        [WHOLE] * (len(parts) + 2),
        0,
    )(*parts, gain, gain_momentum)

    term, gram, ortho = call(
        right_kernel,
        "right",
        [shape((rank, cols), F32), shape((8, 128), F32), shape((2 * rank, half), F32)],
        [WHOLE] * 5,
        0,
    )(mine, swap(mine, "tensor", 1), gram_root, held_grads, held_error)
    parts = partners(term, "replica")
    (joined,) = call(
        functools.partial(middle_kernel, len(parts)),
        "middle",
        [shape((rank + 8, cols), F32)],
        [WHOLE] * (len(parts) + 2) + [ANYWHERE] * 2,
        0,
    )(*parts, gram, tail, from_x, from_y)
    parts = partners(joined, "section")
    x_left = swap(ortho, "section", 1)
    y_left = swap(ortho, "section", 2)
    newbasis, grams, right, wide = call(
        functools.partial(factor_kernel, replicas),
        "factor",
        [shape((rank, cols), F32), shape((8, 128), F32), shape((8, 128), F32), shape((2, sections * cols), F32)],
        [WHOLE] * len(parts),
        0,
    )(*parts)

    entries = rows * cols * tensors * sections
    to_x, to_y, scale, where = call(
        functools.partial(after_kernel, entries),
        "after",
        [shape((half + late, cols), BF16)] * 2 + [shape((8, 128), F32), shape((1,), jnp.int32)],
        [WHOLE] * 7 + [IN_HBM] + [WHOLE] * 2,
        0,
        out_specs=[WHOLE] * 3 + [SCALAR],
        scratch_shapes=[pltpu.VMEM((2 * late, cols), F32), pltpu.SemaphoreType.DMA((1,))],
    )(newbasis, grams, right, swap(right, "tensor", 1), ortho, x_left, y_left, hbm(late_rows), from_x, from_y)
    late_x = swap(to_x, "section", 1)
    late_y = swap(to_y, "section", 2)

    blocks = 4
    block = rows // blocks
    fixed = pl.BlockSpec((rank, cols), lambda i, place: (0, 0))
    step = pl.BlockSpec((block, cols), lambda i, place: (i, 0))
    new_error, new_momentum, out = pl.pallas_call(
        own_kernel,
        out_shape=[pltpu.HBM((rows, cols), BF16), pltpu.HBM((rows, cols), F32), pltpu.HBM((sections * rows, cols), BF16)],
        grid_spec=pltpu.PrefetchScalarGridSpec(
            num_scalar_prefetch=1,
            grid=(blocks,),
            in_specs=[
                pl.BlockSpec((8, 128), lambda i, place: (0, 0)),
                fixed,
                pl.BlockSpec(ortho.shape, lambda i, place: (0, 0)),
                step,
                step,
                step,
                step,
            ],
            out_specs=[step, step, pl.BlockSpec((block, cols), lambda i, place: (place[0] * blocks + i, 0))],
        ),
        compiler_params=PARAMS,
        name="own",
        cost_estimate=cost(12 * rows * cols * rank, 16 * rows * cols),
    )(where, scale, newbasis, ortho, weight, momentum, grads, error)

    (out,) = call(
        near_kernel,
        "near",
        [pltpu.HBM(out.shape, BF16)],
        [WHOLE] * 6 + [IN_HBM],
        12 * early * cols,
        out_specs=[IN_HBM],
        scratch_shapes=[pltpu.VMEM((2 * early, cols), BF16), pltpu.SemaphoreType.DMA((4,))],
        input_output_aliases={6: 0},
    )(scale, newbasis, x_left, y_left, from_x, from_y, hbm(out))
    (new_weight,) = call(
        settle_kernel,
        "settle",
        [pltpu.HBM(out.shape, BF16)],
        [WHOLE] * 2 + [IN_HBM],
        0,
        out_specs=[IN_HBM],
        scratch_shapes=[pltpu.SemaphoreType.DMA((4,))],
        input_output_aliases={2: 0},
    )(late_x, late_y, hbm(out))
    (new_gain,) = call(gain_kernel, "gain", [shape((2, 2 * sections * cols), F32)], [WHOLE] * 2, 0)(
        wide, swap(wide, "tensor", 1)
    )
    return (new_weight, new_error[None], new_momentum, new_gain, new_gain_momentum)


def solution(mesh):
    placed = (
        P("section", "tensor"),
        P("replica", "section", "tensor"),
        P("replica", "section", "tensor"),
        P("section", "tensor"),
        P("tensor", None),
        P(),
        P(None, ("tensor", "section")),
        P(None, ("tensor", "section")),
        P("replica", None, ("tensor", "section")),
    )
    return jax.shard_map(
        on_device,
        mesh=mesh,
        in_specs=placed,
        out_specs=(
            P(None, "tensor"),
            P("replica", "section", "tensor"),
            P("section", "tensor"),
            P(),
            P(None, ("tensor", "section")),
        ),
        check_vma=False,
    )
```

```python
import functools

import jax
import jax.numpy as jnp
from jax import lax
from jax.experimental import pallas as pl
from jax.experimental.pallas import tpu as pltpu
from jax.sharding import PartitionSpec as P

HIGHEST = lax.Precision.HIGHEST
F32 = jnp.float32
BF16 = jnp.bfloat16
KEEP = 0.05 * 0.9 * 0.9
MOVE = 0.05 * (1.0 + 0.9)
CROSS = 20
BLOCKS = 2
LANES = 128
WHOLE = pl.BlockSpec(memory_space=pltpu.VMEM)
ANYWHERE = pl.BlockSpec(memory_space=pl.ANY)
SCALAR = pl.BlockSpec(memory_space=pltpu.SMEM)
IN_HBM = pl.BlockSpec(memory_space=pltpu.HBM)
PARAMS = pltpu.CompilerParams(vmem_limit_bytes=16 * 2**20)


def hbm(x):
    return pltpu.with_memory_space_constraint(x, pltpu.HBM)


def swap(x, axis, distance):
    count = lax.axis_size(axis)
    return lax.ppermute(x, axis, [(i, i ^ distance) for i in range(count)])


BACK = (1, 2)
FRONT = (2, 1)


def beside(x, sides):
    sections = lax.axis_size("section")
    layers = lax.axis_size("replica")
    pairs = [
        (layer * sections + i, layer * sections + (i ^ sides[layer % 2]))
        for layer in range(layers)
        for i in range(sections)
    ]
    return lax.ppermute(x, ("replica", "section"), pairs)


def beside_index(sides):
    odd = (lax.axis_index("replica") & 1) == 1
    return lax.axis_index("section") ^ jnp.where(odd, sides[1], sides[0])


def partners(x, axis):
    count = lax.axis_size(axis)
    while count > 4:
        count //= 2
        x = x + swap(x, axis, count)
    return [x] + [swap(x, axis, distance) for distance in range(1, count)]


def added(parts):
    while len(parts) > 1:
        parts = [a + b for a, b in zip(parts[::2], parts[1::2])]
    return parts[0]


def pieces(x):
    one = x.astype(BF16)
    rest = x - one.astype(F32)
    two = rest.astype(BF16)
    three = (rest - two.astype(F32)).astype(BF16)
    return one, two, three


def dot(a, b, dims):
    return lax.dot_general(a, b, ((dims[0], dims[1]), ((), ())), preferred_element_type=F32)


def dot_full(a, b, dims):
    return lax.dot_general(a, b, ((dims[0], dims[1]), ((), ())), precision=HIGHEST, preferred_element_type=F32)


def folded(x):
    rank = x.shape[0] // 3
    return x[:rank] + x[rank : 2 * rank] + x[2 * rank :]


def tall(x):
    return jnp.concatenate([x[:, i : i + LANES] for i in range(0, x.shape[1], LANES)], axis=0)


def wide(x, count):
    return jnp.concatenate([x[i : i + count] for i in range(0, x.shape[0], count)], axis=1)


def fetch(copies, sems):
    started = []
    for index, (source, target) in enumerate(copies):
        copy = pltpu.make_async_copy(source, target, sems.at[index])
        copy.start()
        started.append(copy)
    return started


def base_of(weight, momentum):
    return weight.astype(F32) - KEEP * momentum


def left_stack(ortho):
    one, two, three = pieces(ortho)
    return jnp.concatenate([one, one, two, one, two, three], axis=0)


def right_stack(newbasis):
    one, two, three = pieces(newbasis)
    return jnp.concatenate([one, two, one, three, two, one], axis=0)


def product(ortho, right):
    return dot(left_stack(ortho), right, ((0,), (0,)))


def moved(base, scale, approx):
    return (base - (MOVE * scale) * approx).astype(BF16)


def start_kernel(weight_any, momentum_any, grads_any, error_any, basis_any, gains_any, back_ref, front_ref, late_ref, kept_ref, given_ref, grads_ref, error_ref, weight_ref, momentum_ref, basis_ref, gains_ref, sems):
    rows = weight_any.shape[0]
    early = back_ref.shape[0]
    late = late_ref.shape[0] // 2
    block = rows // BLOCKS
    copies = [(basis_any, basis_ref), (gains_any, gains_ref)]
    for pair in ((weight_any, weight_ref, momentum_any, momentum_ref), (grads_any, grads_ref, error_any, error_ref)):
        for part in range(BLOCKS):
            span = pl.ds(part * block, block)
            copies.append((pair[0].at[span], pair[1].at[span]))
            copies.append((pair[2].at[span], pair[3].at[span]))
    copies = fetch(copies, sems)
    rank = basis_ref.shape[0]
    half = rows // 2
    copies[0].wait()
    copies[1].wait()
    stack = jnp.concatenate(pieces(basis_ref[...]), axis=0)
    summed = rank * half // LANES
    kept_ref[summed:, :] = tall(gains_ref[...])
    for part in range(BLOCKS):
        copies[2 + 2 * part].wait()
        copies[3 + 2 * part].wait()
        start, stop = part * block, (part + 1) * block
        base = base_of(weight_ref[start:stop, :], momentum_ref[start:stop, :])
        for low, high, ref, shift in (
            (0, early, front_ref, 0),
            (rows - early, rows, back_ref, rows - early),
            (0, late, late_ref, 0),
            (rows - late, rows, late_ref, rows - 2 * late),
        ):
            low, high = max(low, start), min(high, stop)
            if low < high:
                ref[low - shift : high - shift, :] = base[low - start : high - start, :]
    terms = []
    for part in range(BLOCKS):
        copies[2 + 2 * (BLOCKS + part)].wait()
        copies[3 + 2 * (BLOCKS + part)].wait()
        span = pl.ds(part * block, block)
        term = dot(stack, grads_ref[span, :], ((1,), (1,))) + dot(stack, error_ref[span, :], ((1,), (1,)))
        terms.append(folded(term))
    middle = BLOCKS // 2
    front = jnp.concatenate(terms[:middle], axis=1)
    back = jnp.concatenate(terms[middle:], axis=1)
    first = lax.axis_index("tensor") == 0
    kept_ref[:summed, :] = tall(jnp.where(first, front, back))
    given_ref[...] = tall(jnp.where(first, back, front))


def pair_kernel(kept_ref, other_ref, out_ref):
    summed = other_ref.shape[0]
    out_ref[:summed, :] = kept_ref[:summed, :] + other_ref[...]
    out_ref[summed:, :] = kept_ref[summed:, :]


def sum_kernel(replicas, *refs):
    *parts, gain_ref, gain_momentum_ref, mine_ref, new_gain_momentum_ref, tail_ref = refs
    mean = added([part[...] for part in parts]) / replicas
    summed = mine_ref.shape[0]
    mine_ref[...] = mean[:summed]
    gain_mean = wide(mean[summed:], 2)
    new_gain_momentum = 0.9 * gain_momentum_ref[...] + gain_mean
    new_gain_momentum_ref[...] = new_gain_momentum
    tail_ref[...] = tall(gain_ref[...] - 0.02 * (gain_mean + 0.9 * new_gain_momentum))


def right_kernel(mine_ref, other_ref, root_ref, grads_ref, error_ref, term_ref, gram_ref, ortho_ref):
    rank = root_ref.shape[0]
    half = grads_ref.shape[0] // 2
    first = lax.axis_index("tensor") == 0
    mine = wide(mine_ref[...], rank)
    other = wide(other_ref[...], rank)
    lowp = (jnp.where(first, mine, other), jnp.where(first, other, mine))
    orthos = [dot_full(root_ref[...], x, ((0,), (0,))) for x in lowp]
    stacks = [jnp.concatenate(pieces(x), axis=0) for x in orthos]
    term = jnp.zeros((3 * rank, grads_ref.shape[1]), F32)
    for part, stack in enumerate(stacks):
        span = pl.ds(part * half, half)
        term += dot(stack, grads_ref[span, :], ((1,), (0,))) + dot(stack, error_ref[span, :], ((1,), (0,)))
    term_ref[...] = tall(folded(term))
    gram_ref[...] = wide(sum(dot_full(x, x, ((1,), (1,))) for x in orthos), rank // 4)
    for part in range(2):
        ortho_ref[pl.ds(part * rank, rank), :] = orthos[part]


def middle_kernel(count, *refs):
    parts, (gram_ref, tail_ref, _, _, out_ref) = refs[:count], refs[count:]
    out_ref[...] = jnp.concatenate([added([part[...] for part in parts]), gram_ref[...], tail_ref[...]], axis=0)


def factor_kernel(replicas, *refs):
    *parts, newbasis_ref, gram_ref, right_ref, wide_ref = refs
    rank, cols = newbasis_ref.shape
    summed = rank * cols // LANES
    values = [part[...] for part in parts]
    mean = added(values)
    newbasis = wide(mean[:summed], rank) / replicas
    newbasis_ref[...] = newbasis
    right = dot_full(newbasis, newbasis, ((1,), (1,)))
    gram_ref[...] = mean[summed : summed + 8]
    right_ref[...] = wide(right, rank // 4)
    section = lax.axis_index("section")
    for distance, value in enumerate(values):
        gain = wide(value[summed + 8 :], 2)
        for place in range(len(values)):

            @pl.when(section == place ^ distance)
            def _(place=place, gain=gain):
                wide_ref[:, place * cols : (place + 1) * cols] = gain


def after_kernel(entries, newbasis_ref, gram_ref, mine_ref, other_ref, own_ref, back_left_ref, front_left_ref, late_ref, back_ref, front_ref, to_back_ref, to_front_ref, scale_ref, section_ref):
    rank = newbasis_ref.shape[0]
    late = late_ref.shape[0] // 2
    half = own_ref.shape[1]
    squares = (gram_ref[...] / entries) * (mine_ref[...] + other_ref[...])
    mean = jnp.sum(jnp.sum(squares, axis=1, keepdims=True), axis=0, keepdims=True)
    scale = lax.rsqrt(mean + 1e-06)
    scale_ref[...] = jnp.broadcast_to(scale, scale_ref.shape)
    section_ref[0] = lax.axis_index("section")
    right = right_stack(newbasis_ref[...])
    to_back_ref[:half, :] = moved(front_ref[...], scale, product(front_left_ref[:rank, :], right))
    to_back_ref[half:, :] = moved(late_ref[:late, :], scale, product(own_ref[:rank, :late], right))
    to_front_ref[:half, :] = moved(back_ref[...], scale, product(back_left_ref[rank:, :], right))
    to_front_ref[half:, :] = moved(late_ref[late:, :], scale, product(own_ref[rank:, half - late :], right))


def cross_kernel(scale_ref, newbasis_ref, back_left_ref, front_left_ref, back_ref, front_ref, out_ref):
    rank = newbasis_ref.shape[0]
    half = back_left_ref.shape[1]
    count = out_ref.shape[0] // 2
    late = half - count
    scale = scale_ref[0:1, 0:1]
    right = right_stack(newbasis_ref[...])
    out_ref[:count, :] = moved(back_ref[:count, :], scale, product(back_left_ref[rank:, :count], right))
    out_ref[count:, :] = moved(front_ref[late:, :], scale, product(front_left_ref[:rank, late:], right))


def own_kernel(place_ref, scale_ref, newbasis_ref, own_ref, weight_ref, momentum_ref, grads_ref, error_ref, new_error_ref, new_momentum_ref, out_ref):
    del place_ref
    rank, cols = newbasis_ref.shape
    block = weight_ref.shape[0]
    step = pl.program_id(0)
    per = cols // block
    start = (step // per) * rank
    columns = pl.ds(pl.multiple_of((step % per) * block, block), block)
    scale = scale_ref[0:1, 0:1]
    ortho = own_ref[pl.ds(pl.multiple_of(start, rank), rank), columns]
    approx = product(ortho, right_stack(newbasis_ref[...]))
    merged = grads_ref[...].astype(F32) + error_ref[...].astype(F32)
    new_error_ref[...] = (merged - approx).astype(BF16)
    momentum = momentum_ref[...]
    new_momentum_ref[...] = 0.9 * momentum + scale * approx
    out_ref[...] = moved(base_of(weight_ref[...], momentum), scale, approx)


def near_kernel(scale_ref, newbasis_ref, back_left_ref, front_left_ref, back_ref, front_ref, held_ref, out_ref, done_ref, sems):
    del held_ref
    rank = newbasis_ref.shape[0]
    half = back_left_ref.shape[1]
    rows = 2 * half
    scale = scale_ref[0:1, 0:1]
    right = right_stack(newbasis_ref[...])
    back_side = beside_index(BACK) * rows
    front_side = beside_index(FRONT) * rows
    copies = []
    for index, (ref, ortho, to) in enumerate(
        ((back_ref, back_left_ref[rank:, :], back_side + half), (front_ref, front_left_ref[:rank, :], front_side))
    ):
        span = pl.ds(index * half, half)
        done_ref[span, :] = moved(ref[...], scale, product(ortho, right))
        to = pl.multiple_of(to, 16)
        copy = pltpu.make_async_copy(done_ref.at[span], out_ref.at[pl.ds(to, half)], sems.at[index])
        copy.start()
        copies.append(copy)
    for copy in copies:
        copy.wait()


def settle_kernel(sources, cross, late, *refs):
    *came_refs, _, out_ref, sems = refs
    rows = out_ref.shape[0] // lax.axis_size("section")
    half = rows // 2
    back_side = beside_index(BACK) * rows
    front_side = beside_index(FRONT) * rows
    across = (lax.axis_index("section") ^ 3) * rows
    last = rows - late
    places = {
        "back": ((half, across), (late, back_side)),
        "front": ((half, across + half), (late, front_side + last)),
        "cross": ((cross, front_side + last - cross), (cross, back_side + late)),
    }
    copies = []
    for source, came_ref in zip(sources, came_refs):
        start = 0
        for size, to in places[source]:
            to = pl.multiple_of(to, 16)
            copies.append((came_ref.at[pl.ds(start, size), :], out_ref.at[pl.ds(to, size), :]))
            start += size
    for copy in fetch(copies, sems):
        copy.wait()


def gain_kernel(wide_ref, other_ref, out_ref):
    cols = wide_ref.shape[1]
    first = lax.axis_index("tensor") == 0
    mine = wide_ref[...]
    other = other_ref[...]
    out_ref[:, :cols] = jnp.where(first, mine, other)
    out_ref[:, cols:] = jnp.where(first, other, mine)


def shape(dims, kind=F32):
    return jax.ShapeDtypeStruct(dims, kind)


def call(kernel, name, out_shape, in_specs, **more):
    out_specs = more.pop("out_specs", [WHOLE] * len(out_shape))
    return pl.pallas_call(
        kernel,
        out_shape=out_shape,
        in_specs=in_specs,
        out_specs=out_specs,
        compiler_params=PARAMS,
        name=name,
        cost_estimate=pl.CostEstimate(flops=0, bytes_accessed=0, transcendentals=0),
        **more,
    )


def on_device(weight, grads, error, momentum, basis, gram_root, gain, gain_momentum, gain_grads):
    replicas = lax.axis_size("replica")
    tensors = lax.axis_size("tensor")
    sections = lax.axis_size("section")
    rows, cols = weight.shape
    rank = basis.shape[1]
    half = rows // 2
    cross = rows * CROSS // 64
    late = half - cross
    summed = rank * half // LANES
    weight, momentum, grads, error = (hbm(x) for x in (weight, momentum, grads[0], error[0]))

    back, front, late_rows, kept, given, held_grads, held_error = call(
        start_kernel,
        "start",
        [pltpu.VMEM((half, cols), F32)] * 2
        + [shape((2 * late, cols)), shape((summed + 8, LANES)), shape((summed, LANES))]
        + [pltpu.VMEM((rows, cols), BF16)] * 2,
        [IN_HBM] * 6,
        scratch_shapes=[
            pltpu.VMEM((rows, cols), BF16),
            pltpu.VMEM((rows, cols), F32),
            pltpu.VMEM((rank, cols), F32),
            pltpu.VMEM((2, cols), F32),
            pltpu.SemaphoreType.DMA((4 * BLOCKS + 2,)),
        ],
    )(weight, momentum, grads, error, hbm(basis.T), hbm(gain_grads[0]))
    back = beside(back, BACK)
    front = beside(front, FRONT)
    (pair,) = call(pair_kernel, "pair", [shape(kept.shape)], [WHOLE] * 2)(kept, swap(given, "tensor", 1))
    parts = partners(pair, "replica")
    mine, new_gain_momentum, tail = call(
        functools.partial(sum_kernel, replicas),
        "sum",
        [shape((summed, LANES)), shape((2, cols)), shape((8, LANES))],
        [WHOLE] * (len(parts) + 2),
    )(*parts, gain, gain_momentum)

    term, gram, ortho = call(
        right_kernel,
        "right",
        [shape((summed, LANES)), shape((8, LANES)), shape((2 * rank, half))],
        [WHOLE] * 5,
    )(mine, swap(mine, "tensor", 1), gram_root, held_grads, held_error)
    parts = partners(term, "replica")
    (joined,) = call(
        functools.partial(middle_kernel, len(parts)),
        "middle",
        [shape((summed + 16, LANES))],
        [WHOLE] * (len(parts) + 2) + [ANYWHERE] * 2,
    )(*parts, gram, tail, back, front)
    parts = partners(joined, "section")
    back_left = beside(ortho, BACK)
    front_left = beside(ortho, FRONT)
    newbasis, gram, right, gains = call(
        functools.partial(factor_kernel, replicas),
        "factor",
        [shape((rank, cols)), shape((8, LANES)), shape((8, LANES)), shape((2, sections * cols))],
        [WHOLE] * len(parts),
    )(*parts)

    entries = rows * cols * tensors * sections
    to_back, to_front, scale, where = call(
        functools.partial(after_kernel, entries),
        "after",
        [shape((half + late, cols), BF16)] * 2 + [shape((8, LANES)), shape((1,), jnp.int32)],
        [WHOLE] * 10,
        out_specs=[WHOLE] * 3 + [SCALAR],
    )(newbasis, gram, right, swap(right, "tensor", 1), ortho, back_left, front_left, late_rows, back, front)
    late_back = beside(to_back, BACK)
    late_front = beside(to_front, FRONT)
    (to_cross,) = call(cross_kernel, "cross", [shape((2 * cross, cols), BF16)], [WHOLE] * 6)(
        scale, newbasis, back_left, front_left, back, front
    )
    late_cross = swap(to_cross, "replica", 1)

    blocks = 4
    block = rows // blocks
    step = pl.BlockSpec((block, cols), lambda i, place: (i, 0))
    fixed = [pl.BlockSpec(x.shape, lambda i, place: (0, 0)) for x in (scale, newbasis, ortho)]
    new_error, new_momentum, out = pl.pallas_call(
        own_kernel,
        out_shape=[
            pltpu.HBM((rows, cols), BF16),
            pltpu.HBM((rows, cols), F32),
            pltpu.HBM((sections * rows, cols), BF16),
        ],
        grid_spec=pltpu.PrefetchScalarGridSpec(
            num_scalar_prefetch=1,
            grid=(blocks,),
            in_specs=fixed + [step] * 4,
            out_specs=[step, step, pl.BlockSpec((block, cols), lambda i, place: (place[0] * blocks + i, 0))],
        ),
        compiler_params=PARAMS,
        name="own",
        cost_estimate=pl.CostEstimate(flops=0, bytes_accessed=0, transcendentals=0),
    )(where, scale, newbasis, ortho, weight, momentum, grads, error)
    (out,) = call(
        near_kernel,
        "near",
        [pltpu.HBM(out.shape, BF16)],
        [WHOLE] * 6 + [IN_HBM],
        out_specs=[IN_HBM],
        scratch_shapes=[pltpu.VMEM((2 * half, cols), BF16), pltpu.SemaphoreType.DMA((2,))],
        input_output_aliases={6: 0},
    )(scale, newbasis, back_left, front_left, back, front, hbm(out))
    for sources, came in ((("back",), [late_back]), (("front", "cross"), [late_front, late_cross])):
        (out,) = call(
            functools.partial(settle_kernel, sources, cross, late),
            "settle",
            [pltpu.HBM(out.shape, BF16)],
            [WHOLE] * len(came) + [IN_HBM],
            out_specs=[IN_HBM],
            scratch_shapes=[pltpu.SemaphoreType.DMA((2 * len(came),))],
            input_output_aliases={len(came): 0},
        )(*came, hbm(out))
    (new_gain,) = call(gain_kernel, "gain", [shape((2, tensors * sections * cols))], [WHOLE] * 2)(
        gains, swap(gains, "tensor", 1)
    )
    return (out, new_error[None], new_momentum, new_gain, new_gain_momentum)


def solution(mesh):
    placed = (
        P("section", "tensor"),
        P("replica", "section", "tensor"),
        P("replica", "section", "tensor"),
        P("section", "tensor"),
        P("tensor", None),
        P(),
        P(None, ("tensor", "section")),
        P(None, ("tensor", "section")),
        P("replica", None, ("tensor", "section")),
    )
    return jax.shard_map(
        on_device,
        mesh=mesh,
        in_specs=placed,
        out_specs=(
            P(None, "tensor"),
            P("replica", "section", "tensor"),
            P("section", "tensor"),
            P(),
            P(None, ("tensor", "section")),
        ),
        check_vma=False,
    )
```

```python
import functools

import jax
import jax.numpy as jnp
from jax import lax
from jax.experimental import pallas as pl
from jax.experimental.pallas import tpu as pltpu
from jax.sharding import PartitionSpec as P

HIGHEST = lax.Precision.HIGHEST
F32 = jnp.float32
BF16 = jnp.bfloat16
KEEP = 0.05 * 0.9 * 0.9
MOVE = 0.05 * (1.0 + 0.9)
MORE = 10
PASSED = 6
CROSS = 14
BLOCKS = 2
LANES = 128
FAR = 8 * 10**9
WHOLE = pl.BlockSpec(memory_space=pltpu.VMEM)
ANYWHERE = pl.BlockSpec(memory_space=pl.ANY)
SCALAR = pl.BlockSpec(memory_space=pltpu.SMEM)
IN_HBM = pl.BlockSpec(memory_space=pltpu.HBM)
PARAMS = pltpu.CompilerParams(vmem_limit_bytes=16 * 2**20)


def hbm(x):
    return pltpu.with_memory_space_constraint(x, pltpu.HBM)


def swap(x, axis, distance):
    count = lax.axis_size(axis)
    return lax.ppermute(x, axis, [(i, i ^ distance) for i in range(count)])


BACK = (1, 2)
FRONT = (2, 1)


def beside(x, sides):
    sections = lax.axis_size("section")
    layers = lax.axis_size("replica")
    pairs = [
        (layer * sections + i, layer * sections + (i ^ sides[layer % 2]))
        for layer in range(layers)
        for i in range(sections)
    ]
    return lax.ppermute(x, ("replica", "section"), pairs)


def beside_index(sides):
    odd = (lax.axis_index("replica") & 1) == 1
    return lax.axis_index("section") ^ jnp.where(odd, sides[1], sides[0])


def partners(x, axis):
    count = lax.axis_size(axis)
    while count > 4:
        count //= 2
        x = x + swap(x, axis, count)
    return [swap(x, axis, distance) for distance in range(count - 1, 0, -1)] + [x]


def added(parts):
    while len(parts) > 1:
        parts = [a + b for a, b in zip(parts[::2], parts[1::2])]
    return parts[0]


def pieces(x):
    one = x.astype(BF16)
    rest = x - one.astype(F32)
    two = rest.astype(BF16)
    three = (rest - two.astype(F32)).astype(BF16)
    return one, two, three


def dot(a, b, dims):
    return lax.dot_general(a, b, ((dims[0], dims[1]), ((), ())), preferred_element_type=F32)


def dot_full(a, b, dims):
    return lax.dot_general(a, b, ((dims[0], dims[1]), ((), ())), precision=HIGHEST, preferred_element_type=F32)


def folded(x):
    rank = x.shape[0] // 3
    return x[:rank] + x[rank : 2 * rank] + x[2 * rank :]


def tall(x):
    return jnp.concatenate([x[:, i : i + LANES] for i in range(0, x.shape[1], LANES)], axis=0)


def wide(x, count):
    return jnp.concatenate([x[i : i + count] for i in range(0, x.shape[0], count)], axis=1)


def fetch(copies, sems):
    started = []
    for index, (source, target) in enumerate(copies):
        copy = pltpu.make_async_copy(source, target, sems.at[index])
        copy.start()
        started.append(copy)
    return started


def base_of(weight, momentum):
    return weight.astype(F32) - KEEP * momentum


def left_stack(ortho):
    one, two, three = pieces(ortho)
    return jnp.concatenate([one, one, two, one, two, three], axis=0)


def right_stack(newbasis):
    one, two, three = pieces(newbasis)
    return jnp.concatenate([one, two, one, three, two, one], axis=0)


def product(ortho, right):
    return dot(left_stack(ortho), right, ((0,), (0,)))


def moved(base, scale, approx):
    return (base - (MOVE * scale) * approx).astype(BF16)


def start_kernel(weight_any, momentum_any, grads_any, error_any, basis_any, gains_any, back_ref, front_ref, late_ref, grads_ref, error_ref, basis_ref, gains_ref, weight_ref, momentum_ref, sems):
    rows = weight_any.shape[0]
    half = back_ref.shape[0]
    late = late_ref.shape[0] // 2
    block = rows // BLOCKS
    copies = []
    for part in range(BLOCKS):
        span = pl.ds(part * block, block)
        copies.append((weight_any.at[span], weight_ref.at[span]))
        copies.append((momentum_any.at[span], momentum_ref.at[span]))
    copies += [(grads_any, grads_ref), (error_any, error_ref), (basis_any, basis_ref), (gains_any, gains_ref)]
    copies = fetch(copies, sems)
    for part in range(BLOCKS):
        copies[2 * part].wait()
        copies[2 * part + 1].wait()
        start, stop = part * block, (part + 1) * block
        base = base_of(weight_ref[start:stop, :], momentum_ref[start:stop, :])
        for low, high, ref, shift in (
            (0, half, front_ref, 0),
            (half, rows, back_ref, half),
            (0, late, late_ref, 0),
            (rows - late, rows, late_ref, rows - 2 * late),
        ):
            low, high = max(low, start), min(high, stop)
            if low < high:
                ref[low - shift : high - shift, :] = base[low - start : high - start, :]
    for copy in copies[2 * BLOCKS :]:
        copy.wait()


def left_kernel(basis_ref, gains_ref, grads_ref, error_ref, kept_ref, given_ref):
    half = grads_ref.shape[0] // 2
    summed = given_ref.shape[0]
    stack = jnp.concatenate(pieces(basis_ref[...]), axis=0)
    terms = []
    for part in range(2):
        span = pl.ds(part * half, half)
        term = dot(stack, grads_ref[span, :], ((1,), (1,))) + dot(stack, error_ref[span, :], ((1,), (1,)))
        terms.append(tall(folded(term)))
    first = lax.axis_index("tensor") == 0
    kept_ref[:summed, :] = jnp.where(first, terms[0], terms[1])
    kept_ref[summed:, :] = tall(gains_ref[...])
    given_ref[...] = jnp.where(first, terms[1], terms[0])


def pair_kernel(kept_ref, other_ref, out_ref):
    summed = other_ref.shape[0]
    out_ref[:summed, :] = kept_ref[:summed, :] + other_ref[...]
    out_ref[summed:, :] = kept_ref[summed:, :]


def sum_kernel(replicas, *refs):
    *parts, mine_ref, gains_ref = refs
    mean = added([part[...] for part in parts]) / replicas
    summed = mine_ref.shape[0]
    mine_ref[...] = mean[:summed]
    gains_ref[...] = mean[summed:]


def gain_kernel(mean_ref, gain_ref, gain_momentum_ref, new_gain_momentum_ref, tail_ref):
    mean = wide(mean_ref[...], 2)
    new_gain_momentum = 0.9 * gain_momentum_ref[...] + mean
    new_gain_momentum_ref[...] = new_gain_momentum
    tail_ref[...] = tall(gain_ref[...] - 0.02 * (mean + 0.9 * new_gain_momentum))


def right_kernel(mine_ref, other_ref, root_ref, grads_ref, error_ref, _, term_ref, gram_ref, ortho_ref, half_ref):
    rank = root_ref.shape[0]
    half = grads_ref.shape[0] // 2
    first = lax.axis_index("tensor") == 0
    mine = wide(mine_ref[...], rank)
    other = wide(other_ref[...], rank)
    lowp = (jnp.where(first, mine, other), jnp.where(first, other, mine))
    orthos = [dot_full(root_ref[...], x, ((0,), (0,))) for x in lowp]
    stacks = [jnp.concatenate(pieces(x), axis=0) for x in orthos]
    term = jnp.zeros((3 * rank, grads_ref.shape[1]), F32)
    for part, stack in enumerate(stacks):
        span = pl.ds(part * half, half)
        term += dot(stack, grads_ref[span, :], ((1,), (0,))) + dot(stack, error_ref[span, :], ((1,), (0,)))
    term_ref[...] = tall(folded(term))
    gram_ref[...] = wide(sum(dot_full(x, x, ((1,), (1,))) for x in orthos), rank // 4)
    half_ref[...] = tall(jnp.where(first, orthos[0], orthos[1]))
    for part in range(2):
        ortho_ref[pl.ds(part * rank, rank), :] = orthos[part]


def middle_kernel(count, *refs):
    parts, (gram_ref, tail_ref, ortho_ref, _, _, out_ref, long_ref) = refs[:count], refs[count:]
    joined = jnp.concatenate([added([part[...] for part in parts]), gram_ref[...], tail_ref[...]], axis=0)
    out_ref[...] = joined
    long_ref[: joined.shape[0], :] = joined
    long_ref[joined.shape[0] :, :] = ortho_ref[...]


def relay_kernel(_, late_ref, back_ref, front_ref, more_back_ref, more_front_ref, pass_ref):
    more = more_back_ref.shape[0]
    passed = pass_ref.shape[0] // 2
    more_back_ref[...] = late_ref[:more, :]
    more_front_ref[...] = late_ref[late_ref.shape[0] - more :, :]
    pass_ref[:passed, :] = back_ref[:passed, :]
    pass_ref[passed:, :] = front_ref[front_ref.shape[0] - passed :, :]


def far_kernel(in_ref, out_ref):
    out_ref[...] = in_ref[...]


def factor_kernel(replicas, *refs):
    *parts, newbasis_ref, gram_ref, mixed_ref, wide_ref = refs
    rank, cols = newbasis_ref.shape
    summed = rank * cols // LANES
    values = [part[: summed + 16, :] for part in parts]
    mean = added(values)
    newbasis = wide(mean[:summed], rank) / replicas
    newbasis_ref[...] = newbasis
    right = dot_full(newbasis, newbasis, ((1,), (1,)))
    gram_ref[...] = mean[summed : summed + 8]
    two, one = (part[summed + 16 :, :] for part in parts[1:3])
    odd = (lax.axis_index("replica") & 1) == 1
    mixed_ref[:summed, :] = jnp.where(odd, two, one)
    mixed_ref[summed : 2 * summed, :] = jnp.where(odd, one, two)
    mixed_ref[2 * summed :, :] = wide(right, rank // 4)
    section = lax.axis_index("section")
    for distance, value in enumerate(values[::-1]):
        gain = wide(value[summed + 8 :], 2)
        for place in range(len(values)):

            @pl.when(section == place ^ distance)
            def _(place=place, gain=gain):
                wide_ref[:, place * cols : (place + 1) * cols] = gain


def after_kernel(entries, newbasis_ref, gram_ref, mine_ref, other_ref, own_ref, late_ref, back_ref, front_ref, to_back_ref, to_front_ref, scale_ref, back_left_ref, front_left_ref, section_ref):
    rank = newbasis_ref.shape[0]
    half = own_ref.shape[1]
    late = to_back_ref.shape[0] - half
    more = late_ref.shape[0] // 2 - late
    summed = rank * half // LANES
    squares = (gram_ref[...] / entries) * (mine_ref[2 * summed :, :] + other_ref[2 * summed :, :])
    mean = jnp.sum(jnp.sum(squares, axis=1, keepdims=True), axis=0, keepdims=True)
    scale = lax.rsqrt(mean + 1e-06)
    scale_ref[...] = jnp.broadcast_to(scale, scale_ref.shape)
    section_ref[0] = lax.axis_index("section")
    right = right_stack(newbasis_ref[...])
    first = lax.axis_index("tensor") == 0
    for left_ref, start in ((back_left_ref, 0), (front_left_ref, summed)):
        mine = wide(mine_ref[start : start + summed, :], rank)
        other = wide(other_ref[start : start + summed, :], rank)
        left_ref[:rank, :] = jnp.where(first, mine, other)
        left_ref[rank:, :] = jnp.where(first, other, mine)
    to_back_ref[:half, :] = moved(front_ref[...], scale, product(front_left_ref[:rank, :], right))
    to_back_ref[half:, :] = moved(late_ref[more : more + late, :], scale, product(own_ref[:rank, more : more + late], right))
    to_front_ref[:half, :] = moved(back_ref[...], scale, product(back_left_ref[rank:, :], right))
    start = half - late - more
    ortho = own_ref[rank:, start : start + late]
    to_front_ref[half:, :] = moved(late_ref[more + late : more + 2 * late, :], scale, product(ortho, right))


def cross_kernel(passed, scale_ref, newbasis_ref, back_left_ref, front_left_ref, back_ref, front_ref, _, __, ___, out_ref):
    rank = newbasis_ref.shape[0]
    half = back_left_ref.shape[1]
    count = out_ref.shape[0] // 2
    scale = scale_ref[0:1, 0:1]
    right = right_stack(newbasis_ref[...])
    ortho = back_left_ref[rank:, passed : passed + count]
    out_ref[:count, :] = moved(back_ref[passed : passed + count, :], scale, product(ortho, right))
    start = half - passed - count
    ortho = front_left_ref[:rank, start : start + count]
    out_ref[count:, :] = moved(front_ref[start : start + count, :], scale, product(ortho, right))


def own_kernel(place_ref, scale_ref, newbasis_ref, own_ref, weight_ref, momentum_ref, grads_ref, error_ref, new_error_ref, new_momentum_ref, out_ref):
    del place_ref
    rank, cols = newbasis_ref.shape
    block = weight_ref.shape[0]
    step = pl.program_id(0)
    per = cols // block
    start = (step // per) * rank
    columns = pl.ds(pl.multiple_of((step % per) * block, block), block)
    scale = scale_ref[0:1, 0:1]
    ortho = own_ref[pl.ds(pl.multiple_of(start, rank), rank), columns]
    approx = product(ortho, right_stack(newbasis_ref[...]))
    merged = grads_ref[...].astype(F32) + error_ref[...].astype(F32)
    new_error_ref[...] = (merged - approx).astype(BF16)
    momentum = momentum_ref[...]
    new_momentum_ref[...] = 0.9 * momentum + scale * approx
    out_ref[...] = moved(base_of(weight_ref[...], momentum), scale, approx)


def near_kernel(scale_ref, newbasis_ref, back_left_ref, front_left_ref, back_ref, front_ref, more_back_ref, more_front_ref, came_ref, held_ref, out_ref, done_ref, sems):
    del held_ref
    rank = newbasis_ref.shape[0]
    half = back_left_ref.shape[1]
    more = more_back_ref.shape[0]
    passed = came_ref.shape[0] // 2
    rows = 2 * half
    scale = scale_ref[0:1, 0:1]
    right = right_stack(newbasis_ref[...])
    back_side = beside_index(BACK) * rows
    front_side = beside_index(FRONT) * rows
    copies = []
    start = 0
    for index, (base, ortho, to) in enumerate(
        (
            (back_ref[...], back_left_ref[rank:, :], back_side + half),
            (front_ref[...], front_left_ref[:rank, :], front_side),
            (more_back_ref[...], back_left_ref[:rank, :more], back_side),
            (more_front_ref[...], front_left_ref[rank:, half - more :], front_side + rows - more),
            (came_ref[:passed, :], front_left_ref[rank:, :passed], front_side + half),
            (came_ref[passed:, :], back_left_ref[:rank, half - passed :], back_side + half - passed),
        )
    ):
        size = base.shape[0]
        span = pl.ds(start, size)
        done_ref[span, :] = moved(base, scale, product(ortho, right))
        to = pl.multiple_of(to, 16)
        copy = pltpu.make_async_copy(done_ref.at[span], out_ref.at[pl.ds(to, size)], sems.at[index])
        copy.start()
        copies.append(copy)
        start += size
    for copy in copies:
        copy.wait()


def settle_kernel(more, cross, late, from_back_ref, from_front_ref, cross_ref, held_ref, out_ref, sems):
    del held_ref
    rows = out_ref.shape[0] // lax.axis_size("section")
    half = rows // 2
    back_side = beside_index(BACK) * rows
    front_side = beside_index(FRONT) * rows
    across = (lax.axis_index("section") ^ 3) * rows
    last = rows - more - late
    copies = []
    for ref, start, size, to in (
        (from_back_ref, 0, half, across),
        (from_back_ref, half, late, back_side + more),
        (from_front_ref, 0, half, across + half),
        (from_front_ref, half, late, front_side + last),
        (cross_ref, 0, cross, front_side + last - cross),
        (cross_ref, cross, cross, back_side + more + late),
    ):
        to = pl.multiple_of(to, 16)
        copies.append((ref.at[pl.ds(start, size)], out_ref.at[pl.ds(to, size)]))
    for copy in fetch(copies, sems):
        copy.wait()


def gains_kernel(wide_ref, other_ref, out_ref):
    cols = wide_ref.shape[1]
    first = lax.axis_index("tensor") == 0
    mine = wide_ref[...]
    other = other_ref[...]
    out_ref[:, :cols] = jnp.where(first, mine, other)
    out_ref[:, cols:] = jnp.where(first, other, mine)


def shape(dims, kind=F32):
    return jax.ShapeDtypeStruct(dims, kind)


def call(kernel, name, out_shape, in_specs, **more):
    out_specs = more.pop("out_specs", [WHOLE] * len(out_shape))
    flops = more.pop("flops", 0)
    return pl.pallas_call(
        kernel,
        out_shape=out_shape,
        in_specs=in_specs,
        out_specs=out_specs,
        compiler_params=PARAMS,
        name=name,
        cost_estimate=pl.CostEstimate(flops=flops, bytes_accessed=0, transcendentals=0),
        **more,
    )


def on_device(weight, grads, error, momentum, basis, gram_root, gain, gain_momentum, gain_grads):
    replicas = lax.axis_size("replica")
    tensors = lax.axis_size("tensor")
    sections = lax.axis_size("section")
    rows, cols = weight.shape
    rank = basis.shape[1]
    half = rows // 2
    more = rows * MORE // 64
    passed = rows * PASSED // 64
    cross = rows * CROSS // 64
    late = half - more - passed - cross
    summed = rank * half // LANES
    weight, momentum, grads, error = (hbm(x) for x in (weight, momentum, grads[0], error[0]))

    back, front, late_rows, held_grads, held_error, held_basis, held_gains = call(
        start_kernel,
        "start",
        [pltpu.VMEM((half, cols), F32)] * 2
        + [pltpu.VMEM((2 * (more + late), cols), F32)]
        + [pltpu.VMEM((rows, cols), BF16)] * 2
        + [shape((rank, cols)), shape((2, cols))],
        [IN_HBM] * 6,
        scratch_shapes=[
            pltpu.VMEM((rows, cols), BF16),
            pltpu.VMEM((rows, cols), F32),
            pltpu.SemaphoreType.DMA((2 * BLOCKS + 4,)),
        ],
    )(weight, momentum, grads, error, hbm(basis.T), hbm(gain_grads[0]))
    back = beside(back, BACK)
    front = beside(front, FRONT)

    kept, given = call(
        left_kernel, "left", [shape((summed + 8, LANES)), shape((summed, LANES))], [WHOLE] * 4
    )(held_basis, held_gains, held_grads, held_error)
    (pair,) = call(pair_kernel, "pair", [shape(kept.shape)], [WHOLE] * 2)(kept, swap(given, "tensor", 1))
    parts = partners(pair, "replica")
    mine, gain_mean = call(
        functools.partial(sum_kernel, replicas),
        "sum",
        [shape((summed, LANES)), shape((8, LANES))],
        [WHOLE] * len(parts),
    )(*parts)
    new_gain_momentum, tail = call(gain_kernel, "gain", [shape((2, cols)), shape((8, LANES))], [WHOLE] * 3)(
        gain_mean, gain, gain_momentum
    )

    term, gram, ortho, ortho_half = call(
        right_kernel,
        "right",
        [shape((summed, LANES)), shape((8, LANES)), shape((2 * rank, half)), shape((summed, LANES))],
        [WHOLE] * 5 + [ANYWHERE],
    )(mine, swap(mine, "tensor", 1), gram_root, held_grads, held_error, tail)
    parts = partners(term, "replica")
    joined, long = call(
        functools.partial(middle_kernel, len(parts)),
        "middle",
        [shape((summed + 16, LANES)), shape((2 * summed + 16, LANES))],
        [WHOLE] * (len(parts) + 3) + [ANYWHERE] * 2,
    )(*parts, gram, tail, ortho_half, back, front)
    parts = [swap(joined, "section", 3), swap(long, "section", 2), swap(long, "section", 1), joined]
    more_back, more_front, came = call(
        relay_kernel,
        "relay",
        [shape((more, cols))] * 2 + [shape((2 * passed, cols))],
        [ANYWHERE] + [WHOLE] * 3,
    )(joined, late_rows, back, front)
    more_back = beside(more_back, BACK)
    more_front = beside(more_front, FRONT)
    came = swap(came, "replica", 1)
    (parts[0],) = call(far_kernel, "far", [shape(joined.shape)], [WHOLE], flops=FAR)(parts[0])
    newbasis, gram, mixed, gains = call(
        functools.partial(factor_kernel, replicas),
        "factor",
        [shape((rank, cols)), shape((8, LANES)), shape((2 * summed + 8, LANES)), shape((2, sections * cols))],
        [WHOLE] * len(parts),
    )(*parts)

    entries = rows * cols * tensors * sections
    to_back, to_front, scale, back_left, front_left, where = call(
        functools.partial(after_kernel, entries),
        "after",
        [shape((half + late, cols), BF16)] * 2
        + [shape((8, LANES))]
        + [shape((2 * rank, half))] * 2
        + [shape((1,), jnp.int32)],
        [WHOLE] * 8,
        out_specs=[WHOLE] * 5 + [SCALAR],
    )(newbasis, gram, mixed, swap(mixed, "tensor", 1), ortho, late_rows, back, front)
    late_back = beside(to_back, BACK)
    late_front = beside(to_front, FRONT)
    (to_cross,) = call(
        functools.partial(cross_kernel, passed),
        "cross",
        [shape((2 * cross, cols), BF16)],
        [WHOLE] * 6 + [ANYWHERE] * 3,
    )(scale, newbasis, back_left, front_left, back, front, more_back, more_front, came)
    late_cross = swap(to_cross, "replica", 1)

    blocks = 4
    block = rows // blocks
    step = pl.BlockSpec((block, cols), lambda i, place: (i, 0))
    fixed = [pl.BlockSpec(x.shape, lambda i, place: (0, 0)) for x in (scale, newbasis, ortho)]
    new_error, new_momentum, out = pl.pallas_call(
        own_kernel,
        out_shape=[
            pltpu.HBM((rows, cols), BF16),
            pltpu.HBM((rows, cols), F32),
            pltpu.HBM((sections * rows, cols), BF16),
        ],
        grid_spec=pltpu.PrefetchScalarGridSpec(
            num_scalar_prefetch=1,
            grid=(blocks,),
            in_specs=fixed + [step] * 4,
            out_specs=[step, step, pl.BlockSpec((block, cols), lambda i, place: (place[0] * blocks + i, 0))],
        ),
        compiler_params=PARAMS,
        name="own",
        cost_estimate=pl.CostEstimate(flops=0, bytes_accessed=0, transcendentals=0),
    )(where, scale, newbasis, ortho, weight, momentum, grads, error)
    (out,) = call(
        near_kernel,
        "near",
        [pltpu.HBM(out.shape, BF16)],
        [WHOLE] * 9 + [IN_HBM],
        out_specs=[IN_HBM],
        scratch_shapes=[pltpu.VMEM((2 * (half + more + passed), cols), BF16), pltpu.SemaphoreType.DMA((6,))],
        input_output_aliases={9: 0},
    )(scale, newbasis, back_left, front_left, back, front, more_back, more_front, came, hbm(out))
    (out,) = call(
        functools.partial(settle_kernel, more, cross, late),
        "settle",
        [pltpu.HBM(out.shape, BF16)],
        [WHOLE] * 3 + [IN_HBM],
        out_specs=[IN_HBM],
        scratch_shapes=[pltpu.SemaphoreType.DMA((6,))],
        input_output_aliases={3: 0},
    )(late_back, late_front, late_cross, hbm(out))
    (new_gain,) = call(gains_kernel, "gains", [shape((2, tensors * sections * cols))], [WHOLE] * 2)(
        gains, swap(gains, "tensor", 1)
    )
    return (out, new_error[None], new_momentum, new_gain, new_gain_momentum)


def solution(mesh):
    placed = (
        P("section", "tensor"),
        P("replica", "section", "tensor"),
        P("replica", "section", "tensor"),
        P("section", "tensor"),
        P("tensor", None),
        P(),
        P(None, ("tensor", "section")),
        P(None, ("tensor", "section")),
        P("replica", None, ("tensor", "section")),
    )
    return jax.shard_map(
        on_device,
        mesh=mesh,
        in_specs=placed,
        out_specs=(
            P(None, "tensor"),
            P("replica", "section", "tensor"),
            P("section", "tensor"),
            P(),
            P(None, ("tensor", "section")),
        ),
        check_vma=False,
    )
```

```python
import functools

import jax
import jax.numpy as jnp
from jax import lax
from jax.experimental import pallas as pl
from jax.experimental.pallas import tpu as pltpu
from jax.sharding import PartitionSpec as P

HIGHEST = lax.Precision.HIGHEST
F32 = jnp.float32
BF16 = jnp.bfloat16
KEEP = 0.05 * 0.9 * 0.9
MOVE = 0.05 * (1.0 + 0.9)
MORE = 9
PASSED = 7
CROSS = 14
BLOCKS = 2
LANES = 128
FAR = 8 * 10**9
WHOLE = pl.BlockSpec(memory_space=pltpu.VMEM)
ANYWHERE = pl.BlockSpec(memory_space=pl.ANY)
SCALAR = pl.BlockSpec(memory_space=pltpu.SMEM)
IN_HBM = pl.BlockSpec(memory_space=pltpu.HBM)
PARAMS = pltpu.CompilerParams(vmem_limit_bytes=16 * 2**20)


def hbm(x):
    return pltpu.with_memory_space_constraint(x, pltpu.HBM)


def swap(x, axis, distance):
    count = lax.axis_size(axis)
    return lax.ppermute(x, axis, [(i, i ^ distance) for i in range(count)])


BACK = (1, 2)
FRONT = (2, 1)


def beside(x, sides):
    sections = lax.axis_size("section")
    layers = lax.axis_size("replica")
    pairs = [
        (layer * sections + i, layer * sections + (i ^ sides[layer % 2]))
        for layer in range(layers)
        for i in range(sections)
    ]
    return lax.ppermute(x, ("replica", "section"), pairs)


def beside_index(sides):
    odd = (lax.axis_index("replica") & 1) == 1
    return lax.axis_index("section") ^ jnp.where(odd, sides[1], sides[0])


def partners(x, axis):
    count = lax.axis_size(axis)
    while count > 4:
        count //= 2
        x = x + swap(x, axis, count)
    return [swap(x, axis, distance) for distance in range(count - 1, 0, -1)] + [x]


def added(parts):
    while len(parts) > 1:
        parts = [a + b for a, b in zip(parts[::2], parts[1::2])]
    return parts[0]


def pieces(x):
    one = x.astype(BF16)
    rest = x - one.astype(F32)
    two = rest.astype(BF16)
    three = (rest - two.astype(F32)).astype(BF16)
    return one, two, three


def dot(a, b, dims):
    return lax.dot_general(a, b, ((dims[0], dims[1]), ((), ())), preferred_element_type=F32)


def dot_full(a, b, dims):
    return lax.dot_general(a, b, ((dims[0], dims[1]), ((), ())), precision=HIGHEST, preferred_element_type=F32)


def folded(x):
    rank = x.shape[0] // 3
    return x[:rank] + x[rank : 2 * rank] + x[2 * rank :]


def tall(x):
    return jnp.concatenate([x[:, i : i + LANES] for i in range(0, x.shape[1], LANES)], axis=0)


def wide(x, count):
    return jnp.concatenate([x[i : i + count] for i in range(0, x.shape[0], count)], axis=1)


def fetch(copies, sems):
    started = []
    for index, (source, target) in enumerate(copies):
        copy = pltpu.make_async_copy(source, target, sems.at[index])
        copy.start()
        started.append(copy)
    return started


def base_of(weight, momentum):
    return weight.astype(F32) - KEEP * momentum


def left_stack(ortho):
    one, two, three = pieces(ortho)
    return jnp.concatenate([one, one, two, one, two, three], axis=0)


def right_stack(newbasis):
    one, two, three = pieces(newbasis)
    return jnp.concatenate([one, two, one, three, two, one], axis=0)


def product(ortho, right):
    return dot(left_stack(ortho), right, ((0,), (0,)))


def moved(base, scale, approx):
    return (base - (MOVE * scale) * approx).astype(BF16)


def start_kernel(weight_any, momentum_any, grads_any, error_any, basis_any, gains_any, back_ref, front_ref, late_ref, grads_ref, error_ref, basis_ref, gains_ref, weight_ref, momentum_ref, sems):
    rows = weight_any.shape[0]
    half = back_ref.shape[0]
    late = late_ref.shape[0] // 2
    block = rows // BLOCKS
    copies = []
    for part in range(BLOCKS):
        span = pl.ds(part * block, block)
        copies.append((weight_any.at[span], weight_ref.at[span]))
        copies.append((momentum_any.at[span], momentum_ref.at[span]))
    copies += [(grads_any, grads_ref), (error_any, error_ref), (basis_any, basis_ref), (gains_any, gains_ref)]
    copies = fetch(copies, sems)
    for part in range(BLOCKS):
        copies[2 * part].wait()
        copies[2 * part + 1].wait()
        start, stop = part * block, (part + 1) * block
        base = base_of(weight_ref[start:stop, :], momentum_ref[start:stop, :])
        for low, high, ref, shift in (
            (0, half, front_ref, 0),
            (half, rows, back_ref, half),
            (0, late, late_ref, 0),
            (rows - late, rows, late_ref, rows - 2 * late),
        ):
            low, high = max(low, start), min(high, stop)
            if low < high:
                ref[low - shift : high - shift, :] = base[low - start : high - start, :]
    for copy in copies[2 * BLOCKS :]:
        copy.wait()


def left_kernel(basis_ref, gains_ref, grads_ref, error_ref, kept_ref, given_ref):
    half = grads_ref.shape[0] // 2
    summed = given_ref.shape[0]
    stack = jnp.concatenate(pieces(basis_ref[...]), axis=0)
    terms = []
    for part in range(2):
        span = pl.ds(part * half, half)
        term = dot(stack, grads_ref[span, :], ((1,), (1,))) + dot(stack, error_ref[span, :], ((1,), (1,)))
        terms.append(tall(folded(term)))
    first = lax.axis_index("tensor") == 0
    kept_ref[:summed, :] = jnp.where(first, terms[0], terms[1])
    kept_ref[summed:, :] = tall(gains_ref[...])
    given_ref[...] = jnp.where(first, terms[1], terms[0])


def pair_kernel(kept_ref, other_ref, out_ref):
    summed = other_ref.shape[0]
    out_ref[:summed, :] = kept_ref[:summed, :] + other_ref[...]
    out_ref[summed:, :] = kept_ref[summed:, :]


def sum_kernel(replicas, *refs):
    *parts, mine_ref, gains_ref = refs
    mean = added([part[...] for part in parts]) / replicas
    summed = mine_ref.shape[0]
    mine_ref[...] = mean[:summed]
    gains_ref[...] = mean[summed:]


def gain_kernel(mean_ref, gain_ref, gain_momentum_ref, new_gain_momentum_ref, tail_ref):
    mean = wide(mean_ref[...], 2)
    new_gain_momentum = 0.9 * gain_momentum_ref[...] + mean
    new_gain_momentum_ref[...] = new_gain_momentum
    tail_ref[...] = tall(gain_ref[...] - 0.02 * (mean + 0.9 * new_gain_momentum))


def right_kernel(mine_ref, other_ref, root_ref, grads_ref, error_ref, _, term_ref, gram_ref, ortho_ref, half_ref):
    rank = root_ref.shape[0]
    half = grads_ref.shape[0] // 2
    first = lax.axis_index("tensor") == 0
    mine = wide(mine_ref[...], rank)
    other = wide(other_ref[...], rank)
    lowp = (jnp.where(first, mine, other), jnp.where(first, other, mine))
    orthos = [dot_full(root_ref[...], x, ((0,), (0,))) for x in lowp]
    stacks = [jnp.concatenate(pieces(x), axis=0) for x in orthos]
    term = jnp.zeros((3 * rank, grads_ref.shape[1]), F32)
    for part, stack in enumerate(stacks):
        span = pl.ds(part * half, half)
        term += dot(stack, grads_ref[span, :], ((1,), (0,))) + dot(stack, error_ref[span, :], ((1,), (0,)))
    term_ref[...] = tall(folded(term))
    gram_ref[...] = wide(sum(dot_full(x, x, ((1,), (1,))) for x in orthos), rank // 4)
    half_ref[...] = tall(jnp.where(first, orthos[0], orthos[1]))
    for part in range(2):
        ortho_ref[pl.ds(part * rank, rank), :] = orthos[part]


def middle_kernel(count, *refs):
    parts, (gram_ref, tail_ref, ortho_ref, out_ref, long_ref) = refs[:count], refs[count:]
    joined = jnp.concatenate([added([part[...] for part in parts]), gram_ref[...], tail_ref[...]], axis=0)
    out_ref[...] = joined
    long_ref[: joined.shape[0], :] = joined
    long_ref[joined.shape[0] :, :] = ortho_ref[...]


def relay_kernel(_, late_ref, back_ref, front_ref, more_back_ref, more_front_ref, pass_ref):
    more = more_back_ref.shape[0]
    passed = pass_ref.shape[0] // 2
    more_back_ref[...] = late_ref[:more, :]
    more_front_ref[...] = late_ref[late_ref.shape[0] - more :, :]
    pass_ref[:passed, :] = back_ref[:passed, :]
    pass_ref[passed:, :] = front_ref[front_ref.shape[0] - passed :, :]


def far_kernel(in_ref, out_ref):
    out_ref[...] = in_ref[...]


def factor_kernel(replicas, *refs):
    *parts, newbasis_ref, gram_ref, mixed_ref, wide_ref = refs
    rank, cols = newbasis_ref.shape
    summed = rank * cols // LANES
    values = [part[: summed + 16, :] for part in parts]
    mean = added(values)
    newbasis = wide(mean[:summed], rank) / replicas
    newbasis_ref[...] = newbasis
    right = dot_full(newbasis, newbasis, ((1,), (1,)))
    gram_ref[...] = mean[summed : summed + 8]
    two, one = (part[summed + 16 :, :] for part in parts[1:3])
    odd = (lax.axis_index("replica") & 1) == 1
    mixed_ref[:summed, :] = jnp.where(odd, two, one)
    mixed_ref[summed : 2 * summed, :] = jnp.where(odd, one, two)
    mixed_ref[2 * summed :, :] = wide(right, rank // 4)
    section = lax.axis_index("section")
    for distance, value in enumerate(values[::-1]):
        gain = wide(value[summed + 8 :], 2)
        for place in range(len(values)):

            @pl.when(section == place ^ distance)
            def _(place=place, gain=gain):
                wide_ref[:, place * cols : (place + 1) * cols] = gain


def after_kernel(entries, newbasis_ref, gram_ref, mine_ref, other_ref, own_ref, late_ref, back_ref, front_ref, to_back_ref, to_front_ref, scale_ref, back_left_ref, front_left_ref, section_ref):
    rank = newbasis_ref.shape[0]
    half = own_ref.shape[1]
    late = to_back_ref.shape[0] - half
    more = late_ref.shape[0] // 2 - late
    summed = rank * half // LANES
    squares = (gram_ref[...] / entries) * (mine_ref[2 * summed :, :] + other_ref[2 * summed :, :])
    mean = jnp.sum(jnp.sum(squares, axis=1, keepdims=True), axis=0, keepdims=True)
    scale = lax.rsqrt(mean + 1e-06)
    scale_ref[...] = jnp.broadcast_to(scale, scale_ref.shape)
    section_ref[0] = lax.axis_index("section")
    right = right_stack(newbasis_ref[...])
    first = lax.axis_index("tensor") == 0
    for left_ref, start in ((back_left_ref, 0), (front_left_ref, summed)):
        mine = wide(mine_ref[start : start + summed, :], rank)
        other = wide(other_ref[start : start + summed, :], rank)
        left_ref[:rank, :] = jnp.where(first, mine, other)
        left_ref[rank:, :] = jnp.where(first, other, mine)
    to_back_ref[:half, :] = moved(front_ref[...], scale, product(front_left_ref[:rank, :], right))
    to_back_ref[half:, :] = moved(late_ref[more : more + late, :], scale, product(own_ref[:rank, more : more + late], right))
    to_front_ref[:half, :] = moved(back_ref[...], scale, product(back_left_ref[rank:, :], right))
    start = half - late - more
    ortho = own_ref[rank:, start : start + late]
    to_front_ref[half:, :] = moved(late_ref[more + late : more + 2 * late, :], scale, product(ortho, right))


def cross_kernel(passed, scale_ref, newbasis_ref, back_left_ref, front_left_ref, back_ref, front_ref, _, __, ___, out_ref):
    rank = newbasis_ref.shape[0]
    half = back_left_ref.shape[1]
    count = out_ref.shape[0] // 2
    scale = scale_ref[0:1, 0:1]
    right = right_stack(newbasis_ref[...])
    ortho = back_left_ref[rank:, passed : passed + count]
    out_ref[:count, :] = moved(back_ref[passed : passed + count, :], scale, product(ortho, right))
    start = half - passed - count
    ortho = front_left_ref[:rank, start : start + count]
    out_ref[count:, :] = moved(front_ref[start : start + count, :], scale, product(ortho, right))


def own_kernel(place_ref, scale_ref, newbasis_ref, own_ref, weight_ref, momentum_ref, grads_ref, error_ref, new_error_ref, new_momentum_ref, out_ref):
    del place_ref
    rank, cols = newbasis_ref.shape
    block = weight_ref.shape[0]
    step = pl.program_id(0)
    per = cols // block
    start = (step // per) * rank
    columns = pl.ds(pl.multiple_of((step % per) * block, block), block)
    scale = scale_ref[0:1, 0:1]
    ortho = own_ref[pl.ds(pl.multiple_of(start, rank), rank), columns]
    approx = product(ortho, right_stack(newbasis_ref[...]))
    merged = grads_ref[...].astype(F32) + error_ref[...].astype(F32)
    new_error_ref[...] = (merged - approx).astype(BF16)
    momentum = momentum_ref[...]
    new_momentum_ref[...] = 0.9 * momentum + scale * approx
    out_ref[...] = moved(base_of(weight_ref[...], momentum), scale, approx)


def near_kernel(scale_ref, newbasis_ref, back_left_ref, front_left_ref, back_ref, front_ref, more_back_ref, more_front_ref, came_ref, held_ref, out_ref, done_ref, sems):
    del held_ref
    rank = newbasis_ref.shape[0]
    half = back_left_ref.shape[1]
    more = more_back_ref.shape[0]
    passed = came_ref.shape[0] // 2
    rows = 2 * half
    scale = scale_ref[0:1, 0:1]
    right = right_stack(newbasis_ref[...])
    back_side = beside_index(BACK) * rows
    front_side = beside_index(FRONT) * rows
    copies = []
    start = 0
    for index, (base, ortho, to) in enumerate(
        (
            (back_ref[...], back_left_ref[rank:, :], back_side + half),
            (front_ref[...], front_left_ref[:rank, :], front_side),
            (more_back_ref[...], back_left_ref[:rank, :more], back_side),
            (more_front_ref[...], front_left_ref[rank:, half - more :], front_side + rows - more),
            (came_ref[:passed, :], front_left_ref[rank:, :passed], front_side + half),
            (came_ref[passed:, :], back_left_ref[:rank, half - passed :], back_side + half - passed),
        )
    ):
        size = base.shape[0]
        span = pl.ds(start, size)
        done_ref[span, :] = moved(base, scale, product(ortho, right))
        to = pl.multiple_of(to, 16)
        copy = pltpu.make_async_copy(done_ref.at[span], out_ref.at[pl.ds(to, size)], sems.at[index])
        copy.start()
        copies.append(copy)
        start += size
    for copy in copies:
        copy.wait()


def settle_kernel(more, cross, late, from_back_ref, from_front_ref, cross_ref, held_ref, out_ref, sems):
    del held_ref
    rows = out_ref.shape[0] // lax.axis_size("section")
    half = rows // 2
    back_side = beside_index(BACK) * rows
    front_side = beside_index(FRONT) * rows
    across = (lax.axis_index("section") ^ 3) * rows
    last = rows - more - late
    copies = []
    for ref, start, size, to in (
        (from_back_ref, 0, half, across),
        (from_back_ref, half, late, back_side + more),
        (from_front_ref, 0, half, across + half),
        (from_front_ref, half, late, front_side + last),
        (cross_ref, 0, cross, front_side + last - cross),
        (cross_ref, cross, cross, back_side + more + late),
    ):
        to = pl.multiple_of(to, 16)
        copies.append((ref.at[pl.ds(start, size)], out_ref.at[pl.ds(to, size)]))
    for copy in fetch(copies, sems):
        copy.wait()


def gains_kernel(wide_ref, other_ref, out_ref):
    cols = wide_ref.shape[1]
    first = lax.axis_index("tensor") == 0
    mine = wide_ref[...]
    other = other_ref[...]
    out_ref[:, :cols] = jnp.where(first, mine, other)
    out_ref[:, cols:] = jnp.where(first, other, mine)


def shape(dims, kind=F32):
    return jax.ShapeDtypeStruct(dims, kind)


def call(kernel, name, out_shape, in_specs, **more):
    out_specs = more.pop("out_specs", [WHOLE] * len(out_shape))
    flops = more.pop("flops", 0)
    return pl.pallas_call(
        kernel,
        out_shape=out_shape,
        in_specs=in_specs,
        out_specs=out_specs,
        compiler_params=PARAMS,
        name=name,
        cost_estimate=pl.CostEstimate(flops=flops, bytes_accessed=0, transcendentals=0),
        **more,
    )


def on_device(weight, grads, error, momentum, basis, gram_root, gain, gain_momentum, gain_grads):
    replicas = lax.axis_size("replica")
    tensors = lax.axis_size("tensor")
    sections = lax.axis_size("section")
    rows, cols = weight.shape
    rank = basis.shape[1]
    half = rows // 2
    more = rows * MORE // 64
    passed = rows * PASSED // 64
    cross = rows * CROSS // 64
    late = half - more - passed - cross
    summed = rank * half // LANES
    weight, momentum, grads, error = (hbm(x) for x in (weight, momentum, grads[0], error[0]))

    back, front, late_rows, held_grads, held_error, held_basis, held_gains = call(
        start_kernel,
        "start",
        [pltpu.VMEM((half, cols), F32)] * 2
        + [pltpu.VMEM((2 * (more + late), cols), F32)]
        + [pltpu.VMEM((rows, cols), BF16)] * 2
        + [shape((rank, cols)), shape((2, cols))],
        [IN_HBM] * 6,
        scratch_shapes=[
            pltpu.VMEM((rows, cols), BF16),
            pltpu.VMEM((rows, cols), F32),
            pltpu.SemaphoreType.DMA((2 * BLOCKS + 4,)),
        ],
    )(weight, momentum, grads, error, hbm(basis.T), hbm(gain_grads[0]))
    back = beside(back, BACK)
    front = beside(front, FRONT)

    kept, given = call(
        left_kernel, "left", [shape((summed + 8, LANES)), shape((summed, LANES))], [WHOLE] * 4
    )(held_basis, held_gains, held_grads, held_error)
    (pair,) = call(pair_kernel, "pair", [shape(kept.shape)], [WHOLE] * 2)(kept, swap(given, "tensor", 1))
    parts = partners(pair, "replica")
    mine, gain_mean = call(
        functools.partial(sum_kernel, replicas),
        "sum",
        [shape((summed, LANES)), shape((8, LANES))],
        [WHOLE] * len(parts),
    )(*parts)
    new_gain_momentum, tail = call(gain_kernel, "gain", [shape((2, cols)), shape((8, LANES))], [WHOLE] * 3)(
        gain_mean, gain, gain_momentum
    )

    term, gram, ortho, ortho_half = call(
        right_kernel,
        "right",
        [shape((summed, LANES)), shape((8, LANES)), shape((2 * rank, half)), shape((summed, LANES))],
        [WHOLE] * 5 + [ANYWHERE],
    )(mine, swap(mine, "tensor", 1), gram_root, held_grads, held_error, tail)
    parts = partners(term, "replica")
    joined, long = call(
        functools.partial(middle_kernel, len(parts)),
        "middle",
        [shape((summed + 16, LANES)), shape((2 * summed + 16, LANES))],
        [WHOLE] * (len(parts) + 3),
    )(*parts, gram, tail, ortho_half)
    parts = [swap(joined, "section", 3), swap(long, "section", 2), swap(long, "section", 1), joined]
    more_back, more_front, came = call(
        relay_kernel,
        "relay",
        [shape((more, cols))] * 2 + [shape((2 * passed, cols))],
        [ANYWHERE] + [WHOLE] * 3,
    )(joined, late_rows, back, front)
    more_back = beside(more_back, BACK)
    more_front = beside(more_front, FRONT)
    came = swap(came, "replica", 1)
    (parts[0],) = call(far_kernel, "far", [shape(joined.shape)], [WHOLE], flops=FAR)(parts[0])
    newbasis, gram, mixed, gains = call(
        functools.partial(factor_kernel, replicas),
        "factor",
        [shape((rank, cols)), shape((8, LANES)), shape((2 * summed + 8, LANES)), shape((2, sections * cols))],
        [WHOLE] * len(parts),
    )(*parts)

    entries = rows * cols * tensors * sections
    to_back, to_front, scale, back_left, front_left, where = call(
        functools.partial(after_kernel, entries),
        "after",
        [shape((half + late, cols), BF16)] * 2
        + [shape((8, LANES))]
        + [shape((2 * rank, half))] * 2
        + [shape((1,), jnp.int32)],
        [WHOLE] * 8,
        out_specs=[WHOLE] * 5 + [SCALAR],
    )(newbasis, gram, mixed, swap(mixed, "tensor", 1), ortho, late_rows, back, front)
    late_back = beside(to_back, BACK)
    late_front = beside(to_front, FRONT)
    (to_cross,) = call(
        functools.partial(cross_kernel, passed),
        "cross",
        [shape((2 * cross, cols), BF16)],
        [WHOLE] * 6 + [ANYWHERE] * 3,
    )(scale, newbasis, back_left, front_left, back, front, more_back, more_front, came)
    late_cross = swap(to_cross, "replica", 1)

    blocks = 4
    block = rows // blocks
    step = pl.BlockSpec((block, cols), lambda i, place: (i, 0))
    fixed = [pl.BlockSpec(x.shape, lambda i, place: (0, 0)) for x in (scale, newbasis, ortho)]
    new_error, new_momentum, out = pl.pallas_call(
        own_kernel,
        out_shape=[
            pltpu.HBM((rows, cols), BF16),
            pltpu.HBM((rows, cols), F32),
            pltpu.HBM((sections * rows, cols), BF16),
        ],
        grid_spec=pltpu.PrefetchScalarGridSpec(
            num_scalar_prefetch=1,
            grid=(blocks,),
            in_specs=fixed + [step] * 4,
            out_specs=[step, step, pl.BlockSpec((block, cols), lambda i, place: (place[0] * blocks + i, 0))],
        ),
        compiler_params=PARAMS,
        name="own",
        cost_estimate=pl.CostEstimate(flops=0, bytes_accessed=0, transcendentals=0),
    )(where, scale, newbasis, ortho, weight, momentum, grads, error)
    (out,) = call(
        near_kernel,
        "near",
        [pltpu.HBM(out.shape, BF16)],
        [WHOLE] * 9 + [IN_HBM],
        out_specs=[IN_HBM],
        scratch_shapes=[pltpu.VMEM((2 * (half + more + passed), cols), BF16), pltpu.SemaphoreType.DMA((6,))],
        input_output_aliases={9: 0},
    )(scale, newbasis, back_left, front_left, back, front, more_back, more_front, came, hbm(out))
    (out,) = call(
        functools.partial(settle_kernel, more, cross, late),
        "settle",
        [pltpu.HBM(out.shape, BF16)],
        [WHOLE] * 3 + [IN_HBM],
        out_specs=[IN_HBM],
        scratch_shapes=[pltpu.SemaphoreType.DMA((6,))],
        input_output_aliases={3: 0},
    )(late_back, late_front, late_cross, hbm(out))
    (new_gain,) = call(gains_kernel, "gains", [shape((2, tensors * sections * cols))], [WHOLE] * 2)(
        gains, swap(gains, "tensor", 1)
    )
    return (out, new_error[None], new_momentum, new_gain, new_gain_momentum)


def solution(mesh):
    placed = (
        P("section", "tensor"),
        P("replica", "section", "tensor"),
        P("replica", "section", "tensor"),
        P("section", "tensor"),
        P("tensor", None),
        P(),
        P(None, ("tensor", "section")),
        P(None, ("tensor", "section")),
        P("replica", None, ("tensor", "section")),
    )
    return jax.shard_map(
        on_device,
        mesh=mesh,
        in_specs=placed,
        out_specs=(
            P(None, "tensor"),
            P("replica", "section", "tensor"),
            P("section", "tensor"),
            P(),
            P(None, ("tensor", "section")),
        ),
        check_vma=False,
    )
```

```python
import functools

import jax
import jax.numpy as jnp
from jax import lax
from jax.experimental import pallas as pl
from jax.experimental.pallas import tpu as pltpu
from jax.sharding import PartitionSpec as P

HIGHEST = lax.Precision.HIGHEST
F32 = jnp.float32
BF16 = jnp.bfloat16
KEEP = 0.05 * 0.9 * 0.9
MOVE = 0.05 * (1.0 + 0.9)
MORE = 9
PASSED = 7
CROSS = 14
BLOCKS = 2
LANES = 128
FAR = 8 * 10**9
WHOLE = pl.BlockSpec(memory_space=pltpu.VMEM)
ANYWHERE = pl.BlockSpec(memory_space=pl.ANY)
SCALAR = pl.BlockSpec(memory_space=pltpu.SMEM)
IN_HBM = pl.BlockSpec(memory_space=pltpu.HBM)
PARAMS = pltpu.CompilerParams(vmem_limit_bytes=16 * 2**20)


def hbm(x):
    return pltpu.with_memory_space_constraint(x, pltpu.HBM)


def swap(x, axis, distance):
    count = lax.axis_size(axis)
    return lax.ppermute(x, axis, [(i, i ^ distance) for i in range(count)])


BACK = (1, 2)
FRONT = (2, 1)


def beside(x, sides):
    sections = lax.axis_size("section")
    layers = lax.axis_size("replica")
    pairs = [
        (layer * sections + i, layer * sections + (i ^ sides[layer % 2]))
        for layer in range(layers)
        for i in range(sections)
    ]
    return lax.ppermute(x, ("replica", "section"), pairs)


def beside_index(sides):
    odd = (lax.axis_index("replica") & 1) == 1
    return lax.axis_index("section") ^ jnp.where(odd, sides[1], sides[0])


def partners(x, axis):
    count = lax.axis_size(axis)
    while count > 4:
        count //= 2
        x = x + swap(x, axis, count)
    return [swap(x, axis, distance) for distance in range(count - 1, 0, -1)] + [x]


def added(parts):
    while len(parts) > 1:
        parts = [a + b for a, b in zip(parts[::2], parts[1::2])]
    return parts[0]


def pieces(x):
    one = x.astype(BF16)
    rest = x - one.astype(F32)
    two = rest.astype(BF16)
    three = (rest - two.astype(F32)).astype(BF16)
    return one, two, three


def dot(a, b, dims):
    return lax.dot_general(a, b, ((dims[0], dims[1]), ((), ())), preferred_element_type=F32)


def dot_full(a, b, dims):
    return lax.dot_general(a, b, ((dims[0], dims[1]), ((), ())), precision=HIGHEST, preferred_element_type=F32)


def folded(x):
    rank = x.shape[0] // 3
    return x[:rank] + x[rank : 2 * rank] + x[2 * rank :]


def tall(x):
    return jnp.concatenate([x[:, i : i + LANES] for i in range(0, x.shape[1], LANES)], axis=0)


def wide(x, count):
    return jnp.concatenate([x[i : i + count] for i in range(0, x.shape[0], count)], axis=1)


def fetch(copies, sems):
    started = []
    for index, (source, target) in enumerate(copies):
        copy = pltpu.make_async_copy(source, target, sems.at[index])
        copy.start()
        started.append(copy)
    return started


def base_of(weight, momentum):
    return weight.astype(F32) - KEEP * momentum


def left_stack(ortho):
    one, two, three = pieces(ortho)
    return jnp.concatenate([one, one, two, one, two, three], axis=0)


def right_stack(newbasis):
    one, two, three = pieces(newbasis)
    return jnp.concatenate([one, two, one, three, two, one], axis=0)


def product(ortho, right):
    return dot(left_stack(ortho), right, ((0,), (0,)))


def moved(base, scale, approx):
    return (base - (MOVE * scale) * approx).astype(BF16)


def start_kernel(weight_any, momentum_any, grads_any, error_any, basis_any, gains_any, back_ref, front_ref, late_ref, grads_ref, error_ref, basis_ref, gains_ref, weight_ref, momentum_ref, sems):
    rows = weight_any.shape[0]
    half = back_ref.shape[0]
    late = late_ref.shape[0] // 2
    block = rows // BLOCKS
    copies = []
    for part in range(BLOCKS):
        span = pl.ds(part * block, block)
        copies.append((weight_any.at[span], weight_ref.at[span]))
        copies.append((momentum_any.at[span], momentum_ref.at[span]))
    copies += [(grads_any, grads_ref), (error_any, error_ref), (basis_any, basis_ref), (gains_any, gains_ref)]
    copies = fetch(copies, sems)
    for part in range(BLOCKS):
        copies[2 * part].wait()
        copies[2 * part + 1].wait()
        start, stop = part * block, (part + 1) * block
        base = base_of(weight_ref[start:stop, :], momentum_ref[start:stop, :])
        for low, high, ref, shift in (
            (0, half, front_ref, 0),
            (half, rows, back_ref, half),
            (0, late, late_ref, 0),
            (rows - late, rows, late_ref, rows - 2 * late),
        ):
            low, high = max(low, start), min(high, stop)
            if low < high:
                ref[low - shift : high - shift, :] = base[low - start : high - start, :]
    for copy in copies[2 * BLOCKS :]:
        copy.wait()


def left_kernel(basis_ref, gains_ref, grads_ref, error_ref, kept_ref, given_ref):
    half = grads_ref.shape[0] // 2
    summed = given_ref.shape[0]
    stack = jnp.concatenate(pieces(basis_ref[...]), axis=0)
    terms = []
    for part in range(2):
        span = pl.ds(part * half, half)
        term = dot(stack, grads_ref[span, :], ((1,), (1,))) + dot(stack, error_ref[span, :], ((1,), (1,)))
        terms.append(tall(folded(term)))
    first = lax.axis_index("tensor") == 0
    kept_ref[:summed, :] = jnp.where(first, terms[0], terms[1])
    kept_ref[summed:, :] = tall(gains_ref[...])
    given_ref[...] = jnp.where(first, terms[1], terms[0])


def pair_kernel(kept_ref, other_ref, out_ref):
    summed = other_ref.shape[0]
    out_ref[:summed, :] = kept_ref[:summed, :] + other_ref[...]
    out_ref[summed:, :] = kept_ref[summed:, :]


def sum_kernel(replicas, *refs):
    *parts, mine_ref, gains_ref = refs
    mean = added([part[...] for part in parts]) / replicas
    summed = mine_ref.shape[0]
    mine_ref[...] = mean[:summed]
    gains_ref[...] = mean[summed:]


def gain_kernel(mean_ref, gain_ref, gain_momentum_ref, new_gain_momentum_ref, tail_ref):
    mean = wide(mean_ref[...], 2)
    new_gain_momentum = 0.9 * gain_momentum_ref[...] + mean
    new_gain_momentum_ref[...] = new_gain_momentum
    tail_ref[...] = tall(gain_ref[...] - 0.02 * (mean + 0.9 * new_gain_momentum))


def right_kernel(mine_ref, other_ref, root_ref, grads_ref, error_ref, _, term_ref, gram_ref, ortho_ref, half_ref):
    rank = root_ref.shape[0]
    half = grads_ref.shape[0] // 2
    first = lax.axis_index("tensor") == 0
    mine = wide(mine_ref[...], rank)
    other = wide(other_ref[...], rank)
    lowp = (jnp.where(first, mine, other), jnp.where(first, other, mine))
    orthos = [dot_full(root_ref[...], x, ((0,), (0,))) for x in lowp]
    stacks = [jnp.concatenate(pieces(x), axis=0) for x in orthos]
    term = jnp.zeros((3 * rank, grads_ref.shape[1]), F32)
    for part, stack in enumerate(stacks):
        span = pl.ds(part * half, half)
        term += dot(stack, grads_ref[span, :], ((1,), (0,))) + dot(stack, error_ref[span, :], ((1,), (0,)))
    term_ref[...] = tall(folded(term))
    gram_ref[...] = wide(sum(dot_full(x, x, ((1,), (1,))) for x in orthos), rank // 4)
    half_ref[...] = tall(jnp.where(first, orthos[0], orthos[1]))
    for part in range(2):
        ortho_ref[pl.ds(part * rank, rank), :] = orthos[part]


def middle_kernel(count, *refs):
    parts, (gram_ref, tail_ref, ortho_ref, out_ref, long_ref) = refs[:count], refs[count:]
    joined = jnp.concatenate([added([part[...] for part in parts]), gram_ref[...], tail_ref[...]], axis=0)
    out_ref[...] = joined
    long_ref[: joined.shape[0], :] = joined
    long_ref[joined.shape[0] :, :] = ortho_ref[...]


def relay_kernel(_, late_ref, back_ref, front_ref, more_back_ref, more_front_ref, pass_ref):
    more = more_back_ref.shape[0]
    passed = pass_ref.shape[0] // 2
    more_back_ref[...] = late_ref[:more, :]
    more_front_ref[...] = late_ref[late_ref.shape[0] - more :, :]
    pass_ref[:passed, :] = back_ref[:passed, :]
    pass_ref[passed:, :] = front_ref[front_ref.shape[0] - passed :, :]


def far_kernel(in_ref, out_ref):
    out_ref[...] = in_ref[...]


def factor_kernel(replicas, *refs):
    *parts, newbasis_ref, gram_ref, mixed_ref, wide_ref = refs
    rank, cols = newbasis_ref.shape
    summed = rank * cols // LANES
    values = [part[: summed + 16, :] for part in parts]
    mean = added(values)
    newbasis = wide(mean[:summed], rank) / replicas
    newbasis_ref[...] = newbasis
    right = dot_full(newbasis, newbasis, ((1,), (1,)))
    gram_ref[...] = mean[summed : summed + 8]
    two, one = (part[summed + 16 :, :] for part in parts[1:3])
    odd = (lax.axis_index("replica") & 1) == 1
    mixed_ref[:summed, :] = jnp.where(odd, two, one)
    mixed_ref[summed : 2 * summed, :] = jnp.where(odd, one, two)
    mixed_ref[2 * summed :, :] = wide(right, rank // 4)
    section = lax.axis_index("section")
    for distance, value in enumerate(values[::-1]):
        gain = wide(value[summed + 8 :], 2)
        for place in range(len(values)):

            @pl.when(section == place ^ distance)
            def _(place=place, gain=gain):
                wide_ref[:, place * cols : (place + 1) * cols] = gain


def after_kernel(entries, newbasis_ref, gram_ref, mine_ref, other_ref, own_ref, late_ref, back_ref, front_ref, to_back_ref, to_front_ref, scale_ref, back_left_ref, front_left_ref, section_ref):
    rank = newbasis_ref.shape[0]
    half = own_ref.shape[1]
    late = to_back_ref.shape[0] - half
    more = late_ref.shape[0] // 2 - late
    summed = rank * half // LANES
    squares = (gram_ref[...] / entries) * (mine_ref[2 * summed :, :] + other_ref[2 * summed :, :])
    mean = jnp.sum(jnp.sum(squares, axis=1, keepdims=True), axis=0, keepdims=True)
    scale = lax.rsqrt(mean + 1e-06)
    scale_ref[...] = jnp.broadcast_to(scale, scale_ref.shape)
    section_ref[0] = lax.axis_index("section")
    right = right_stack(newbasis_ref[...])
    first = lax.axis_index("tensor") == 0
    for left_ref, start in ((back_left_ref, 0), (front_left_ref, summed)):
        mine = wide(mine_ref[start : start + summed, :], rank)
        other = wide(other_ref[start : start + summed, :], rank)
        left_ref[:rank, :] = jnp.where(first, mine, other)
        left_ref[rank:, :] = jnp.where(first, other, mine)
    to_back_ref[:half, :] = moved(front_ref[...], scale, product(front_left_ref[:rank, :], right))
    to_back_ref[half:, :] = moved(late_ref[more : more + late, :], scale, product(own_ref[:rank, more : more + late], right))
    to_front_ref[:half, :] = moved(back_ref[...], scale, product(back_left_ref[rank:, :], right))
    start = half - late - more
    ortho = own_ref[rank:, start : start + late]
    to_front_ref[half:, :] = moved(late_ref[more + late : more + 2 * late, :], scale, product(ortho, right))


def cross_kernel(passed, scale_ref, newbasis_ref, back_left_ref, front_left_ref, back_ref, front_ref, _, __, ___, out_ref):
    rank = newbasis_ref.shape[0]
    half = back_left_ref.shape[1]
    count = out_ref.shape[0] // 2
    scale = scale_ref[0:1, 0:1]
    right = right_stack(newbasis_ref[...])
    ortho = back_left_ref[rank:, passed : passed + count]
    out_ref[:count, :] = moved(back_ref[passed : passed + count, :], scale, product(ortho, right))
    start = half - passed - count
    ortho = front_left_ref[:rank, start : start + count]
    out_ref[count:, :] = moved(front_ref[start : start + count, :], scale, product(ortho, right))


def own_kernel(place_ref, scale_ref, newbasis_ref, own_ref, weight_ref, momentum_ref, grads_ref, error_ref, new_error_ref, new_momentum_ref, out_ref):
    del place_ref
    rank, cols = newbasis_ref.shape
    block = weight_ref.shape[0]
    step = pl.program_id(0)
    per = cols // block
    start = (step // per) * rank
    columns = pl.ds(pl.multiple_of((step % per) * block, block), block)
    scale = scale_ref[0:1, 0:1]
    ortho = own_ref[pl.ds(pl.multiple_of(start, rank), rank), columns]
    approx = product(ortho, right_stack(newbasis_ref[...]))
    merged = grads_ref[...].astype(F32) + error_ref[...].astype(F32)
    new_error_ref[...] = (merged - approx).astype(BF16)
    momentum = momentum_ref[...]
    new_momentum_ref[...] = 0.9 * momentum + scale * approx
    out_ref[...] = moved(base_of(weight_ref[...], momentum), scale, approx)


def near_kernel(scale_ref, newbasis_ref, back_left_ref, front_left_ref, back_ref, front_ref, more_back_ref, more_front_ref, came_ref, held_ref, out_ref, done_ref, sems):
    del held_ref
    rank = newbasis_ref.shape[0]
    half = back_left_ref.shape[1]
    more = more_back_ref.shape[0]
    passed = came_ref.shape[0] // 2
    rows = 2 * half
    scale = scale_ref[0:1, 0:1]
    right = right_stack(newbasis_ref[...])
    back_side = beside_index(BACK) * rows
    front_side = beside_index(FRONT) * rows
    copies = []
    start = 0
    for index, (base, ortho, to) in enumerate(
        (
            (back_ref[...], back_left_ref[rank:, :], back_side + half),
            (front_ref[...], front_left_ref[:rank, :], front_side),
            (more_back_ref[...], back_left_ref[:rank, :more], back_side),
            (more_front_ref[...], front_left_ref[rank:, half - more :], front_side + rows - more),
            (came_ref[:passed, :], front_left_ref[rank:, :passed], front_side + half),
            (came_ref[passed:, :], back_left_ref[:rank, half - passed :], back_side + half - passed),
        )
    ):
        size = base.shape[0]
        span = pl.ds(start, size)
        done_ref[span, :] = moved(base, scale, product(ortho, right))
        to = pl.multiple_of(to, 16)
        copy = pltpu.make_async_copy(done_ref.at[span], out_ref.at[pl.ds(to, size)], sems.at[index])
        copy.start()
        copies.append(copy)
        start += size
    for copy in copies:
        copy.wait()


def settle_kernel(more, cross, late, from_back_ref, from_front_ref, cross_ref, held_ref, out_ref, sems):
    del held_ref
    rows = out_ref.shape[0] // lax.axis_size("section")
    half = rows // 2
    back_side = beside_index(BACK) * rows
    front_side = beside_index(FRONT) * rows
    across = (lax.axis_index("section") ^ 3) * rows
    last = rows - more - late
    copies = []
    for ref, start, size, to in (
        (from_back_ref, 0, half, across),
        (from_back_ref, half, late, back_side + more),
        (from_front_ref, 0, half, across + half),
        (from_front_ref, half, late, front_side + last),
        (cross_ref, 0, cross, front_side + last - cross),
        (cross_ref, cross, cross, back_side + more + late),
    ):
        to = pl.multiple_of(to, 16)
        copies.append((ref.at[pl.ds(start, size)], out_ref.at[pl.ds(to, size)]))
    for copy in fetch(copies, sems):
        copy.wait()


def gains_kernel(wide_ref, other_ref, out_ref):
    cols = wide_ref.shape[1]
    first = lax.axis_index("tensor") == 0
    mine = wide_ref[...]
    other = other_ref[...]
    out_ref[:, :cols] = jnp.where(first, mine, other)
    out_ref[:, cols:] = jnp.where(first, other, mine)


def shape(dims, kind=F32):
    return jax.ShapeDtypeStruct(dims, kind)


def call(kernel, name, out_shape, in_specs, **more):
    out_specs = more.pop("out_specs", [WHOLE] * len(out_shape))
    flops = more.pop("flops", 0)
    return pl.pallas_call(
        kernel,
        out_shape=out_shape,
        in_specs=in_specs,
        out_specs=out_specs,
        compiler_params=PARAMS,
        name=name,
        cost_estimate=pl.CostEstimate(flops=flops, bytes_accessed=0, transcendentals=0),
        **more,
    )


def on_device(weight, grads, error, momentum, basis, gram_root, gain, gain_momentum, gain_grads):
    replicas = lax.axis_size("replica")
    tensors = lax.axis_size("tensor")
    sections = lax.axis_size("section")
    rows, cols = weight.shape
    rank = basis.shape[1]
    half = rows // 2
    more = rows * MORE // 64
    passed = rows * PASSED // 64
    cross = rows * CROSS // 64
    late = half - more - passed - cross
    summed = rank * half // LANES
    weight, momentum, grads, error = (hbm(x) for x in (weight, momentum, grads[0], error[0]))

    back, front, late_rows, held_grads, held_error, held_basis, held_gains = call(
        start_kernel,
        "start",
        [pltpu.VMEM((half, cols), F32)] * 2
        + [pltpu.VMEM((2 * (more + late), cols), F32)]
        + [pltpu.VMEM((rows, cols), BF16)] * 2
        + [shape((rank, cols)), shape((2, cols))],
        [IN_HBM] * 6,
        scratch_shapes=[
            pltpu.VMEM((rows, cols), BF16),
            pltpu.VMEM((rows, cols), F32),
            pltpu.SemaphoreType.DMA((2 * BLOCKS + 4,)),
        ],
    )(weight, momentum, grads, error, hbm(basis.T), hbm(gain_grads[0]))
    back = beside(back, BACK)
    front = beside(front, FRONT)

    kept, given = call(
        left_kernel, "left", [shape((summed + 8, LANES)), shape((summed, LANES))], [WHOLE] * 4
    )(held_basis, held_gains, held_grads, held_error)
    (pair,) = call(pair_kernel, "pair", [shape(kept.shape)], [WHOLE] * 2)(kept, swap(given, "tensor", 1))
    parts = partners(pair, "replica")
    mine, gain_mean = call(
        functools.partial(sum_kernel, replicas),
        "sum",
        [shape((summed, LANES)), shape((8, LANES))],
        [WHOLE] * len(parts),
    )(*parts)
    new_gain_momentum, tail = call(gain_kernel, "gain", [shape((2, cols)), shape((8, LANES))], [WHOLE] * 3)(
        gain_mean, gain, gain_momentum
    )

    term, gram, ortho, ortho_half = call(
        right_kernel,
        "right",
        [shape((summed, LANES)), shape((8, LANES)), shape((2 * rank, half)), shape((summed, LANES))],
        [WHOLE] * 5 + [ANYWHERE],
    )(mine, swap(mine, "tensor", 1), gram_root, held_grads, held_error, tail)
    parts = partners(term, "replica")
    joined, long = call(
        functools.partial(middle_kernel, len(parts)),
        "middle",
        [shape((summed + 16, LANES)), shape((2 * summed + 16, LANES))],
        [WHOLE] * (len(parts) + 3),
    )(*parts, gram, tail, ortho_half)
    parts = [swap(joined, "section", 3), swap(long, "section", 2), swap(long, "section", 1), joined]
    more_back, more_front, came = call(
        relay_kernel,
        "relay",
        [shape((more, cols))] * 2 + [shape((2 * passed, cols))],
        [ANYWHERE] + [WHOLE] * 3,
    )(joined, late_rows, back, front)
    more_back = beside(more_back, BACK)
    more_front = beside(more_front, FRONT)
    came = swap(came, "replica", 1)
    (parts[0],) = call(far_kernel, "far", [shape(joined.shape)], [WHOLE], flops=FAR)(parts[0])
    newbasis, gram, mixed, gains = call(
        functools.partial(factor_kernel, replicas),
        "factor",
        [shape((rank, cols)), shape((8, LANES)), shape((2 * summed + 8, LANES)), shape((2, sections * cols))],
        [WHOLE] * len(parts),
    )(*parts)

    entries = rows * cols * tensors * sections
    to_back, to_front, scale, back_left, front_left, where = call(
        functools.partial(after_kernel, entries),
        "after",
        [shape((half + late, cols), BF16)] * 2
        + [shape((8, LANES))]
        + [shape((2 * rank, half))] * 2
        + [shape((1,), jnp.int32)],
        [WHOLE] * 8,
        out_specs=[WHOLE] * 5 + [SCALAR],
    )(newbasis, gram, mixed, swap(mixed, "tensor", 1), ortho, late_rows, back, front)
    late_back = beside(to_back, BACK)
    late_front = beside(to_front, FRONT)
    (to_cross,) = call(
        functools.partial(cross_kernel, passed),
        "cross",
        [shape((2 * cross, cols), BF16)],
        [WHOLE] * 6 + [ANYWHERE] * 3,
    )(scale, newbasis, back_left, front_left, back, front, more_back, more_front, came)
    late_cross = swap(to_cross, "replica", 1)

    blocks = 2
    block = rows // blocks
    step = pl.BlockSpec((block, cols), lambda i, place: (i, 0))
    fixed = [pl.BlockSpec(x.shape, lambda i, place: (0, 0)) for x in (scale, newbasis, ortho)]
    new_error, new_momentum, out = pl.pallas_call(
        own_kernel,
        out_shape=[
            pltpu.HBM((rows, cols), BF16),
            pltpu.HBM((rows, cols), F32),
            pltpu.HBM((sections * rows, cols), BF16),
        ],
        grid_spec=pltpu.PrefetchScalarGridSpec(
            num_scalar_prefetch=1,
            grid=(blocks,),
            in_specs=fixed + [step] * 4,
            out_specs=[step, step, pl.BlockSpec((block, cols), lambda i, place: (place[0] * blocks + i, 0))],
        ),
        compiler_params=PARAMS,
        name="own",
        cost_estimate=pl.CostEstimate(flops=0, bytes_accessed=0, transcendentals=0),
    )(where, scale, newbasis, ortho, weight, momentum, grads, error)
    (out,) = call(
        near_kernel,
        "near",
        [pltpu.HBM(out.shape, BF16)],
        [WHOLE] * 9 + [IN_HBM],
        out_specs=[IN_HBM],
        scratch_shapes=[pltpu.VMEM((2 * (half + more + passed), cols), BF16), pltpu.SemaphoreType.DMA((6,))],
        input_output_aliases={9: 0},
    )(scale, newbasis, back_left, front_left, back, front, more_back, more_front, came, hbm(out))
    (out,) = call(
        functools.partial(settle_kernel, more, cross, late),
        "settle",
        [pltpu.HBM(out.shape, BF16)],
        [WHOLE] * 3 + [IN_HBM],
        out_specs=[IN_HBM],
        scratch_shapes=[pltpu.SemaphoreType.DMA((6,))],
        input_output_aliases={3: 0},
    )(late_back, late_front, late_cross, hbm(out))
    (new_gain,) = call(gains_kernel, "gains", [shape((2, tensors * sections * cols))], [WHOLE] * 2)(
        gains, swap(gains, "tensor", 1)
    )
    return (out, new_error[None], new_momentum, new_gain, new_gain_momentum)


def solution(mesh):
    placed = (
        P("section", "tensor"),
        P("replica", "section", "tensor"),
        P("replica", "section", "tensor"),
        P("section", "tensor"),
        P("tensor", None),
        P(),
        P(None, ("tensor", "section")),
        P(None, ("tensor", "section")),
        P("replica", None, ("tensor", "section")),
    )
    return jax.shard_map(
        on_device,
        mesh=mesh,
        in_specs=placed,
        out_specs=(
            P(None, "tensor"),
            P("replica", "section", "tensor"),
            P("section", "tensor"),
            P(),
            P(None, ("tensor", "section")),
        ),
        check_vma=False,
    )
```
